32 devices in a mesh: sub: 8 (over y, x, core), col: 4 (over z).
Axes of the slice: x: 2, y: 2, z: 4, core: 2. Of those that a mesh axis runs over, the one named last changes fastest.
Arguments:
- perm: float32 [512, 512, 128], P('sub', 'col'), may hold values from 0.1 to 10
- accum: float32 [512, 512, 128], P('sub', 'col'), may hold values from 0.05 to 2
- rhs: float32 [512, 512, 128], P('sub', 'col'), may hold values from -24 to 24
- depth_x: int32 [16, 512], P('sub', 'col'), may hold values from 0 to 4, as said below
- depth_y: int32 [512, 8], P('sub', 'col'), may hold values from 0 to 4, as said below
Outputs:
- pressure: float32 [512, 512, 128], P('sub', 'col')
The draws below stay inside these ranges and needn't reach their ends.
Inputs may be any that keep to these rules, and one draw needn't show every extreme that they name: Both sides of one interface share its depth: depth_x[2 s + 1, j] = depth_x[2 s + 2, j] and depth_y[i, 2 c + 1] = depth_y[i, 2 c + 2]; faces on the grid's boundary have depth 0; the depth 4 occurs. `depth_y`: as for depth_x, along the second dimension.
All inputs are finite; a program needn't handle non-finite values.
Results may differ from the reference program's by a relative error of at most 0.0003.
Values sent between devices are 32-bit elements; how exact they have to be, the bound alone decides.
A program may use at most 192 MiB of HBM per device.

```python
import math
import jax
import jax.numpy as jnp
from jax import lax

SX = 64
SY = 128
NZ = 128
OVL = 4
SWEEPS = 3
ITERS = 2
NX = 512
NY = 512
N_SUB = 8
N_COL = 4


def draw_depth_x(key, part):
    interior_depth = jax.random.randint(jax.random.fold_in(key, 11), (N_SUB - 1, NY), 0, OVL + 1, dtype=jnp.int32)
    interior_depth = interior_depth.at[0, 0].set(OVL)
    boundary = jnp.zeros((1, NY), jnp.int32)
    interfaces = jnp.concatenate([boundary, interior_depth, boundary], axis=0)
    return jnp.stack([interfaces[:-1], interfaces[1:]], axis=1).reshape(2 * N_SUB, NY)


def draw_depth_y(key, part):
    interior_depth = jax.random.randint(jax.random.fold_in(key, 12), (NX, N_COL - 1), 0, OVL + 1, dtype=jnp.int32)
    interior_depth = interior_depth.at[0, 0].set(OVL)
    boundary = jnp.zeros((NX, 1), jnp.int32)
    interfaces = jnp.concatenate([boundary, interior_depth, boundary], axis=1)
    return jnp.stack([interfaces[:, :-1], interfaces[:, 1:]], axis=2).reshape(NX, 2 * N_COL)


def block_scale(key, dims, shards, least, high):
    gain = 1.0
    for dim, parts in shards:
        draws = jax.random.uniform(jax.random.fold_in(jax.random.fold_in(key, 6), dim), (parts,), jnp.float32, least / len(shards), high / len(shards))
        gain = gain * jnp.repeat(jnp.exp(draws), dims[dim] // parts).reshape((-1,) + (1,) * (len(dims) - 1 - dim))
    return gain


def normal_values(stream_key, extent, deviation, limit, shards=(), held_as=jnp.bfloat16):
    result = jax.random.normal(stream_key, extent, jnp.float32) * deviation
    if len(shards) > 0:
        result = block_scale(stream_key, extent, shards, -0.22, 0.18) * result
    return jnp.clip(result, min=-limit, max=limit).astype(held_as)


def setup_inputs(seed: int = 0) -> dict:
    key_list = jax.random.split(jax.random.key(seed), 6)
    perm = jnp.clip(jnp.exp(math.log(10.0) - 4.6051702 * jax.random.uniform(key_list[0], (NX, NY, NZ), jnp.float32) ** block_scale(key_list[0], (NX, NY, NZ), ((0, 8), (1, 4)), -0.2, 0.2)), 0.1, 10.0)
    accum = jnp.clip(jnp.exp(math.log(2.0) - 3.6888794 * jax.random.uniform(key_list[1], (NX, NY, NZ), jnp.float32) ** block_scale(key_list[1], (NX, NY, NZ), ((0, 8), (1, 4)), -0.2, 0.2)), 0.05, 2.0)
    rhs = normal_values(key_list[2], (NX, NY, NZ), 4.0, 24.0, ((0, 8), (1, 4)), jnp.float32)
    depth_x = draw_depth_x(jax.random.fold_in(key_list[5], 71), 0)
    depth_y = draw_depth_y(jax.random.fold_in(key_list[5], 71), 0)
    return {"perm": perm, "accum": accum, "rhs": rhs, "depth_x": depth_x, "depth_y": depth_y}


VERTICAL = 0.1


def harmonic(first_perm, second_perm):
    return 2.0 * first_perm * second_perm / (first_perm + second_perm)


def coefficients(perm_padded, accum_centre, inside_x, inside_y):
    inside = inside_x[:, None, None] & inside_y[None, :, None]
    perm_safe = jnp.where(inside, perm_padded, 1.0)
    across_x = harmonic(perm_safe[:-1, 1:-1], perm_safe[1:, 1:-1])
    open_x = (inside_x[:-1] & inside_x[1:])[:, None, None]
    across_x = jnp.where(open_x, across_x, 0.0)
    across_y = harmonic(perm_safe[1:-1, :-1], perm_safe[1:-1, 1:])
    open_y = (inside_y[:-1] & inside_y[1:])[None, :, None]
    across_y = jnp.where(open_y, across_y, 0.0)
    centre = perm_safe[1:-1, 1:-1]
    upward = VERTICAL * harmonic(centre[:, :, :-1], centre[:, :, 1:])
    bottom = jnp.zeros_like(centre[:, :, :1])
    lower_z = jnp.concatenate([bottom, upward], axis=2)
    upper_z = jnp.concatenate([upward, bottom], axis=2)
    lower_x = across_x[:-1]
    upper_x = across_x[1:]
    lower_y = across_y[:, :-1]
    upper_y = across_y[:, 1:]
    diagonal = accum_centre + lower_x + upper_x + lower_y + upper_y + lower_z + upper_z
    return (diagonal, lower_x, upper_x, lower_y, upper_y, lower_z, upper_z)


def neighbour_sum(padded, coeffs):
    diagonal, lower_x, upper_x, lower_y, upper_y, lower_z, upper_z = coeffs
    centre = padded[1:-1, 1:-1]
    bottom = jnp.zeros_like(centre[:, :, :1])
    below = jnp.concatenate([bottom, centre[:, :, :-1]], axis=2)
    above = jnp.concatenate([centre[:, :, 1:], bottom], axis=2)
    total = lower_x * padded[:-2, 1:-1] + upper_x * padded[2:, 1:-1]
    total = total + lower_y * padded[1:-1, :-2] + upper_y * padded[1:-1, 2:]
    return total + lower_z * below + upper_z * above


def operate(padded, coeffs):
    return coeffs[0] * padded[1:-1, 1:-1] - neighbour_sum(padded, coeffs)


def membership(depth_lo_hi_x, depth_lo_hi_y, inside_x, inside_y, block_x, block_y, margin):
    row_ids = jnp.arange(block_x + 2 * margin, dtype=jnp.int32)[:, None]
    column_ids = jnp.arange(block_y + 2 * margin, dtype=jnp.int32)[None, :]
    in_rows = (row_ids >= margin) & (row_ids < margin + block_x)
    in_columns = (column_ids >= margin) & (column_ids < margin + block_y)
    low_x = jnp.pad(depth_lo_hi_x[0], (margin, margin))[None, :]
    high_x = jnp.pad(depth_lo_hi_x[1], (margin, margin))[None, :]
    low_y = jnp.pad(depth_lo_hi_y[:, 0], (margin, margin))[:, None]
    high_y = jnp.pad(depth_lo_hi_y[:, 1], (margin, margin))[:, None]
    member = in_rows & in_columns
    member = member | ((row_ids < margin) & in_columns & ((margin - 1 - row_ids) < low_x))
    member = member | ((row_ids >= margin + block_x) & in_columns & ((row_ids - margin - block_x) < high_x))
    member = member | ((column_ids < margin) & in_rows & ((margin - 1 - column_ids) < low_y))
    member = member | ((column_ids >= margin + block_y) & in_rows & ((column_ids - margin - block_y) < high_y))
    return member & inside_x[:, None] & inside_y[None, :]


def local_solve(resid_ext, coeffs, diag_safe, member_cells):
    correction = jnp.zeros_like(resid_ext)
    for sweep_index in range(SWEEPS):
        padded = jnp.pad(correction, ((1, 1), (1, 1), (0, 0)))
        correction = jnp.where(member_cells, (resid_ext + neighbour_sum(padded, coeffs)) / diag_safe, 0.0)
    return correction


def reference(perm, accum, rhs, depth_x, depth_y):
    total_x = SX * N_SUB
    total_y = SY * N_COL
    margin = OVL
    grid_x = jnp.arange(total_x + 2, dtype=jnp.int32) - 1
    grid_y = jnp.arange(total_y + 2, dtype=jnp.int32) - 1
    global_coeffs = coefficients(jnp.pad(perm, ((1, 1), (1, 1), (0, 0))), accum,
                                 (grid_x >= 0) & (grid_x < total_x), (grid_y >= 0) & (grid_y < total_y))
    perm_wide = jnp.pad(perm, ((margin + 1, margin + 1), (margin + 1, margin + 1), (0, 0)))
    accum_wide = jnp.pad(accum, ((margin, margin), (margin, margin), (0, 0)))
    ext_x = SX + 2 * margin
    ext_y = SY + 2 * margin
    pressure = jnp.zeros_like(rhs)
    for iteration in range(ITERS):
        if iteration == 0:
            residual = rhs
        else:
            residual = rhs - operate(jnp.pad(pressure, ((1, 1), (1, 1), (0, 0))), global_coeffs)
        resid_wide = jnp.pad(residual, ((margin, margin), (margin, margin), (0, 0)))

        def visit(totals, domain):
            sub_index = domain // N_COL
            col_index = domain % N_COL
            start_x = sub_index * SX
            start_y = col_index * SY
            zero_index = jnp.zeros((), jnp.int32)
            perm_block = lax.dynamic_slice(perm_wide, (start_x, start_y, zero_index), (ext_x + 2, ext_y + 2, NZ))
            accum_block = lax.dynamic_slice(accum_wide, (start_x, start_y, zero_index), (ext_x, ext_y, NZ))
            resid_block = lax.dynamic_slice(resid_wide, (start_x, start_y, zero_index), (ext_x, ext_y, NZ))
            row_global = start_x - (margin + 1) + jnp.arange(ext_x + 2, dtype=jnp.int32)
            column_global = start_y - (margin + 1) + jnp.arange(ext_y + 2, dtype=jnp.int32)
            inside_x = (row_global >= 0) & (row_global < total_x)
            inside_y = (column_global >= 0) & (column_global < total_y)
            coeffs = coefficients(perm_block, accum_block, inside_x, inside_y)
            block_depth_x = lax.dynamic_slice(depth_x, (2 * sub_index, start_y), (2, SY))
            block_depth_y = lax.dynamic_slice(depth_y, (start_x, 2 * col_index), (SX, 2))
            member = membership(block_depth_x, block_depth_y, inside_x[1:-1], inside_y[1:-1], SX, SY, margin)
            member_cells = member[:, :, None]
            diag_safe = jnp.where(member_cells, coeffs[0], 1.0)
            correction = local_solve(resid_block, coeffs, diag_safe, member_cells)
            summed, covered = totals
            previous = lax.dynamic_slice(summed, (start_x, start_y, zero_index), (ext_x, ext_y, NZ))
            summed = lax.dynamic_update_slice(summed, previous + correction, (start_x, start_y, zero_index))
            seen = lax.dynamic_slice(covered, (start_x, start_y), (ext_x, ext_y))
            covered = lax.dynamic_update_slice(covered, seen + member.astype(jnp.float32), (start_x, start_y))
            return (summed, covered), None

        initial = (jnp.zeros((total_x + 2 * margin, total_y + 2 * margin, NZ), jnp.float32),
                   jnp.zeros((total_x + 2 * margin, total_y + 2 * margin), jnp.float32))
        totals, ignored = lax.scan(visit, initial, jnp.arange(N_SUB * N_COL, dtype=jnp.int32))
        summed, covered = totals
        owned_sum = summed[margin:margin + total_x, margin:margin + total_y]
        owned_cover = covered[margin:margin + total_x, margin:margin + total_y]
        pressure = pressure + owned_sum / owned_cover[:, :, None]
    return pressure
```

```python
import functools

import jax
import jax.numpy as jnp
from jax import lax
from jax.experimental import pallas as pl
from jax.experimental.pallas import tpu as pltpu
from jax.sharding import PartitionSpec as P

OVL = 4
VERTICAL = 0.1
MESH = pl.DeviceIdType.MESH

PADX = 3
PADY = 8
DIRS = ((-1, 0), (1, 0), (0, -1), (0, 1), (-1, -1), (-1, 1), (1, -1), (1, 1))
CHUNK = 8


def recip(value):
    return pl.reciprocal(value, approx=True)


def harmonic(first, second):
    return first * second * recip(first + second)


def kernel(n_sub, n_col, bx, by, perm, accum, rhs, depth_x, depth_y, out,
           dx_ref, dy_ref, hx, hy, pm, w, r, b, fx, fy, fz, pr,
           xw, xb, xc, yw, yb, yc, ssem, rsem, lsem):
    nz = 128
    s = lax.axis_index("sub")
    k = lax.axis_index("col")
    ex, ey = bx + 2 * PADX, by + 2 * PADY
    c = pm
    n_a, n_q = bx // 8 - 1, by // 8 + 1
    x_end, y_end = PADX + bx, PADY + by

    def exists(d):
        ok = None
        for coord, step, count in ((s, d[0], n_sub), (k, d[1], n_col)):
            if step == -1:
                test = coord > 0
            elif step == 1:
                test = coord < count - 1
            else:
                continue
            ok = test if ok is None else ok & test
        return ok

    def device(d):
        return (s + d[0], k + d[1])

    own_x, own_y = pl.ds(PADX, bx), pl.ds(PADY, by)

    def local(n):
        here = pl.ds(n * CHUNK, CHUNK)
        there = pl.ds(PADX + n * CHUNK, CHUNK)
        return [pltpu.make_async_copy(src.at[here], dst.at[there, own_y, :], lsem.at[i, n])
                for i, (src, dst) in enumerate(((perm, pm), (accum, w), (rhs, r)))]

    for n in range(bx // CHUNK):
        for copy in local(n):
            copy.start()

    def each(count, body):
        def step(i, carry):
            body(i)
            return carry
        lax.fori_loop(0, count, step, 0)

    def fill(value, *refs):
        for ref in refs:
            for x0 in (0, x_end):
                ref[x0:x0 + PADX, :, :] = jnp.full((PADX, ey, nz), value, jnp.float32)

        def rows(i):
            for ref in refs:
                for y0 in (0, y_end):
                    ref[pl.ds(PADX + 8 * i, 8), y0:y0 + PADY, :] = jnp.full((8, PADY, nz), value, jnp.float32)
        each(bx // 8, rows)

    fill(1.0, pm, w)
    fill(0.0, r, pr)
    hx[...] = jnp.zeros(hx.shape, jnp.int32)
    hy[...] = jnp.zeros(hy.shape, jnp.int32)

    barrier = pltpu.get_barrier_semaphore()
    arrivals = jnp.int32(0)
    for d in DIRS:
        @pl.when(exists(d))
        def _(d=d):
            pl.semaphore_signal(barrier, inc=1, device_id=device(d), device_id_type=MESH)
        arrivals = arrivals + jnp.where(exists(d), 1, 0).astype(jnp.int32)
    pl.semaphore_wait(barrier, arrivals)

    counter = [0]

    def remote(src, dst, d):
        i = counter[0]
        counter[0] += 1
        return d, pltpu.make_async_remote_copy(
            src_ref=src, dst_ref=dst, send_sem=ssem.at[i], recv_sem=rsem.at[i],
            device_id=device(d), device_id_type=MESH)

    def start(copies):
        for d, copy in copies:
            pl.when(exists(d))(copy.start)

    def wait_recv(copies):
        for d, copy in copies:
            pl.when(exists((-d[0], -d[1])))(copy.wait_recv)

    def wait_send(copies):
        for d, copy in copies:
            pl.when(exists(d))(copy.wait_send)

    def halo(src, ox, oy, dst, d, width):
        def span(step, offset, extent, pad, thick):
            if step == 0:
                return pl.ds(offset, extent), pl.ds(pad, extent)
            if step == 1:
                return pl.ds(offset + extent - thick, thick), pl.ds(pad - thick, thick)
            return pl.ds(offset, thick), pl.ds(pad + extent, thick)

        sxs, dxs = span(d[0], ox, bx, PADX, width)
        sys_, dys = span(d[1], oy, by, PADY, width)
        return remote(src.at[sxs, sys_, :], dst.at[dxs, dys, :], d)

    halos = [halo(perm, 0, 0, pm, d, 3) for d in DIRS]
    halos += [halo(accum, 0, 0, w, d, 2) for d in DIRS]
    halos += [halo(rhs, 0, 0, r, d, 2) for d in DIRS]
    halos += [remote(depth_y, hy.at[0], (1, 0)), remote(depth_y, hy.at[1], (-1, 0)),
              remote(depth_x, hx.at[0], (0, 1)), remote(depth_x, hx.at[1], (0, -1))]
    start(halos)

    for ref in (xb, xc):
        ref[0, 6:8] = jnp.zeros((2, ey, nz), jnp.float32)
        ref[1, 0:2] = jnp.zeros((2, ey, nz), jnp.float32)

    def clear(i):
        for ref in (yw, yb, yc):
            for u in range(2):
                ref[u, pl.ds(i * 2, 2)] = jnp.zeros((2, 16, nz), jnp.float32)
    each(ex // 2, clear)

    dx_ref[...] = jnp.zeros(dx_ref.shape, jnp.int32)
    dy_ref[...] = jnp.zeros(dy_ref.shape, jnp.int32)
    for side in range(2):
        dx_ref[side, own_y, :] = jnp.broadcast_to(depth_x[side:side + 1, :], (nz, by)).T
        lanes = jnp.broadcast_to(depth_y[side:side + 1, :], (nz, bx)).T
        dy_ref[side, own_x] = jnp.broadcast_to(lanes[:, None, :], (bx, 8, nz))

    def at(ref, x0, y0, rows=8, columns=8):
        return ref[pl.ds(x0, rows), pl.ds(y0, columns), :]

    def put(ref, x0, y0, value):
        ref[pl.ds(x0, value.shape[0]), pl.ds(y0, value.shape[1]), :] = value

    def strip_x(t):
        return PADX - 2 + t * (bx - 4)

    def strip_y(u):
        return PADY - 4 + u * (by - 8)

    def sublane(rows):
        return lax.broadcasted_iota(jnp.int32, (rows, 8, nz), 1)

    def stencil(ref, x0, y0, rows=8, following=None, lx=0, ly=0):
        wide = at(ref, x0 - lx - 1, y0 - ly, rows + 2)
        centre = wide[1:rows + 1]
        face = at(fx, x0 - 1, y0, rows + 1)
        total = face[0:rows] * wide[0:rows] + face[1:rows + 1] * wide[2:rows + 2]
        low = at(fy, x0, y0, rows)
        total = total + low * at(ref, x0 - lx, y0 - ly - 1, rows)
        back = pltpu.roll(low * centre, 7, 1)
        if following is None:
            total = total + at(fy, x0, y0 + 1, rows) * at(ref, x0 - lx, y0 - ly + 1, rows)
        else:
            total = total + jnp.where(sublane(rows) == 7, following, back)
        up = at(fz, x0, y0, rows)
        total = total + up * pltpu.roll(centre, nz - 1, 2)
        total = total + pltpu.roll(up * centre, 1, 2)
        return total, centre, back

    def coefficients(x0, y0, rows=8, following=None, frame=False):
        wide = 2.0 * at(pm, x0 - 1, y0, rows + 2)
        centre = wide[1:rows + 1]
        across_x = harmonic(wide[0:rows + 1], wide[1:rows + 2])
        across_y0 = harmonic(2.0 * at(pm, x0, y0 - 1, rows), centre)
        lane = lax.broadcasted_iota(jnp.int32, (1, 8, nz), 2)
        scale = jnp.where(lane < nz - 1, jnp.float32(VERTICAL), 0.0)
        up = scale * harmonic(centre, pltpu.roll(centre, nz - 1, 2))
        if following is None:
            across_y1 = harmonic(centre, 2.0 * at(pm, x0, y0 + 1, rows))
        else:
            across_y1 = pltpu.roll(jnp.where(sublane(rows) == 0, following, across_y0), 7, 1)
        if frame:
            row = x0 - 1 + lax.broadcasted_iota(jnp.int32, (rows + 1, 8, nz), 0)
            shut = (row == jnp.where(s == 0, PADX - 1, -1)) | (
                row == jnp.where(s == n_sub - 1, x_end - 1, -1))
            across_x = jnp.where(shut, 0.0, across_x)
            column = y0 + sublane(rows)
            first = jnp.where(k == 0, PADY, -1)
            last = jnp.where(k == n_col - 1, y_end, -1)
            across_y0 = jnp.where((column == first) | (column == last), 0.0, across_y0)
            across_y1 = jnp.where((column + 1 == first) | (column + 1 == last), 0.0, across_y1)
        put(fx, x0 - 1, y0, across_x)
        put(fy, x0, y0, across_y0)
        put(fz, x0, y0, up)
        faces = (across_x[0:rows] + across_x[1:rows + 1] + across_y0 + across_y1
                 + up + pltpu.roll(up, 1, 2))
        inverse = recip(at(w, x0, y0, rows) + faces)
        if not frame:
            put(w, x0, y0, inverse)
            put(b, x0, y0, inverse * at(r, x0, y0, rows))
        return inverse, across_y0

    def end_y(t, u):
        return jnp.where(t == 0, hy[0, pl.ds(u, 1), bx - 1:bx], hy[1, pl.ds(u, 1), 0:1])[None]

    def end_x(u, t):
        return jnp.where(u == 0, hx[0, pl.ds(t, 1), by - 1:by], hx[1, pl.ds(t, 1), 0:1])[None]

    def frame_block(x0, y0, rows, t, u, first):
        if first:
            inverse, _ = coefficients(x0, y0, rows, frame=True)
            i = x0 - PADX + lax.broadcasted_iota(jnp.int32, (rows, 8, nz), 0)
            j = y0 - PADY + sublane(rows)
            in_x, in_y = (i >= 0) & (i < bx), (j >= 0) & (j < by)
            member = in_x & in_y
            if t is not None:
                m = jnp.where(t == 0, i, bx - 1 - i)
                deep = dx_ref[t, pl.ds(y0, 8), :][None]
                member = member | ((m < 0) & (-1 - m < deep))
                other = ((m < 0) & in_y) | ((m >= 0) & (m < deep))
                if u is not None:
                    edge = end_y(t, u)
                    other = other | ((m == -1) & (j == jnp.where(u == 0, -1, by)) & (edge >= 1))
                weight_x = jnp.where(other, inverse, 0.0)
                put(xw.at[t], x0 - strip_x(t), y0, weight_x)
            if u is not None:
                m_y = jnp.where(u == 0, j, by - 1 - j)
                deep = dy_ref[u, pl.ds(x0, rows), :, :]
                member = member | ((m_y < 0) & (-1 - m_y < deep))
                other = ((m_y < 0) & in_x) | ((m_y >= 0) & (m_y < deep))
                if t is not None:
                    edge = end_x(u, t)
                    other = other | ((m_y == -1) & (i == jnp.where(t == 0, -1, bx)) & (edge >= 1))
                weight_y = jnp.where(other, inverse, 0.0)
                put(yw.at[u], x0, y0 - strip_y(u), weight_y)
            weight = jnp.where(member, inverse, 0.0)
            put(w, x0, y0, weight)
            source = at(r, x0, y0, rows)
            put(b, x0, y0, weight * source)
            if t is not None:
                put(xb.at[t], x0 - strip_x(t), y0, weight_x * source)
            if u is not None:
                put(yb.at[u], x0, y0 - strip_y(u), weight_y * source)
            return
        total, centre, _ = stencil(pr, x0, y0, rows)
        total = at(r, x0, y0, rows) + total

        def restarted(weight):
            return jnp.where(weight > 0.0, weight * total - centre, 0.0)

        put(b, x0, y0, restarted(at(w, x0, y0, rows)))
        if t is not None:
            lx = strip_x(t)
            put(xb.at[t], x0 - lx, y0, restarted(at(xw.at[t], x0 - lx, y0, rows)))
        if u is not None:
            ly = strip_y(u)
            put(yb.at[u], x0, y0 - ly, restarted(at(yw.at[u], x0, y0 - ly, rows)))

    def row(a):
        return PADX + 4 + 8 * a

    def column(q):
        return PADY - 4 + 8 * q

    def frame(first):
        unroll = 5 if (n_q - 2) % 5 == 0 else 1

        def along_x(n):
            t, q = n // ((n_q - 2) // unroll), n % ((n_q - 2) // unroll)
            for v in range(unroll):
                frame_block(PADX - 2 + t * (bx - 2), column(1 + q * unroll + v), 6, t, None, first)
        each(2 * ((n_q - 2) // unroll), along_x)

        def along_y(u):
            for a in range(n_a):
                frame_block(row(a), column(u * (n_q - 1)), 8, None, u, first)
        each(2, along_y)

        def corner(n):
            t, u = n // 2, n % 2
            frame_block(PADX - 2 + t * (bx - 2), column(u * (n_q - 1)), 6, t, u, first)
        each(4, corner)

    def chain(body, columns, *args):
        following = None
        for q in reversed(columns):
            following = body(*args, q, following)

    def second(x0, rows, q, following):
        y0 = column(q)
        total, _, back = stencil(b, x0, y0, rows, following)
        put(c, x0, y0, at(b, x0, y0, rows) + at(w, x0, y0, rows) * total)
        return back

    def second_inner():
        each(n_a - 2, lambda a: chain(second, range(2, n_q - 2), row(a + 1), 8))

    def second_outer():
        def ends(a):
            chain(second, range(n_q - 2, n_q), row(a + 1), 8)
            chain(second, range(0, 2), row(a + 1), 8)
        each(n_a - 2, ends)
        each(2, lambda t: chain(second, range(n_q), PADX + 4 + t * (bx - 16), 8))
        each(2, lambda t: chain(second, range(n_q), PADX - 1 + t * (bx - 3), 5))

    def second_strips():
        def along_x(t):
            lx = strip_x(t)
            x0 = PADX - 1 + t * (bx - 3)
            src, dst, weight = xb.at[t], xc.at[t], xw.at[t]

            def block(q, following):
                y0 = column(q)
                total, _, back = stencil(src, x0, y0, 5, following, lx, 0)
                put(dst, x0 - lx, y0, at(src, x0 - lx, y0, 5) + at(weight, x0 - lx, y0, 5) * total)
                return back
            chain(block, range(n_q))
        each(2, along_x)

        def along_y(u):
            ly = strip_y(u)
            y0 = PADY - 3 + u * (by - 2)
            src, dst, weight = yb.at[u], yc.at[u], yw.at[u]
            for a in range(bx // 8):
                x0 = PADX + 8 * a
                total, _, _ = stencil(src, x0, y0, 8, None, 0, ly)
                put(dst, x0, y0 - ly, at(src, x0, y0 - ly) + at(weight, x0, y0 - ly) * total)
        each(2, along_y)

    def finish(turn, x0, y0, value):
        if turn == 0:
            put(pr, x0, y0, value)
        else:
            put(out, x0 - PADX, y0 - PADY, at(pr, x0, y0, value.shape[0]) + value)

    def third(x0, y0, rows, following):
        total, _, back = stencil(c, x0, y0, rows, following)
        return at(b, x0, y0, rows) + at(w, x0, y0, rows) * total, back

    def third_inner(turn):
        def block(x0, q, following):
            y0 = PADY + 8 * q
            value, back = third(x0, y0, 8, following)
            finish(turn, x0, y0, value)
            return back
        each(n_a, lambda a: chain(block, range(1, by // 8 - 1), row(a)))

    def border(turn, x0, y0, rows, t, u, following=(None, None)):
        total, back = third(x0, y0, rows, following[0])
        cover = jnp.ones(total.shape, jnp.float32)
        back_x = None
        if t is not None:
            lx = strip_x(t)
            weight = at(xw.at[t], x0 - lx, y0, rows)
            others, _, back_x = stencil(xc.at[t], x0, y0, rows, following[1], lx, 0)
            total = total + (at(xb.at[t], x0 - lx, y0, rows) + weight * others)
            cover = jnp.where(weight > 0.0, cover + 1.0, cover)
        if u is not None:
            ly = strip_y(u)
            weight = at(yw.at[u], x0, y0 - ly, rows)
            others, _, _ = stencil(yc.at[u], x0, y0, rows, None, 0, ly)
            total = total + (at(yb.at[u], x0, y0 - ly, rows) + weight * others)
            cover = jnp.where(weight > 0.0, cover + 1.0, cover)
        finish(turn, x0, y0, total * recip(cover))
        return back, back_x

    def third_border(turn):
        def corner(n):
            t, u = n // 2, n % 2
            border(turn, PADX + t * (bx - 4), PADY + u * (by - 8), 4, t, u)
        each(4, corner)

        def along_x(t):
            following = (None, None)
            for q in reversed(range(1, by // 8 - 1)):
                following = border(turn, PADX + t * (bx - 4), PADY + 8 * q, 4, t, None, following)
        each(2, along_x)

        def along_y(u):
            for a in range(n_a):
                border(turn, row(a), PADY + u * (by - 8), 8, None, u)
        each(2, along_y)

    for copy in local(0):
        copy.wait()

    def first_row(a):
        for copy in local(a + 1):
            copy.wait()
        following = None
        for q in reversed(range(1, n_q - 1)):
            _, following = coefficients(row(a), column(q), following=following)
    each(n_a, first_row)
    second_inner()
    wait_recv(halos)
    frame(True)
    second_outer()
    second_strips()
    third_border(0)
    spread = [halo(pr, PADX, PADY, pr, d, 3) for d in DIRS]
    start(spread)
    third_inner(0)

    def restart_row(a):
        following = None
        for q in reversed(range(1, n_q - 1)):
            x0, y0 = row(a), column(q)
            total, centre, following = stencil(pr, x0, y0, 8, following)
            put(b, x0, y0, at(w, x0, y0) * (at(r, x0, y0) + total) - centre)
    each(n_a, restart_row)
    second_inner()
    wait_recv(spread)
    frame(False)
    second_outer()
    second_strips()
    third_border(1)
    third_inner(1)
    wait_send(halos)
    wait_send(spread)


def store(source, target, sem):
    rows = source.shape[0] // 8
    copies = [pltpu.make_async_copy(source.at[pl.ds(i * rows, rows)], target.at[pl.ds(i * rows, rows)], sem.at[i])
              for i in range(8)]
    for copy in copies:
        copy.start()
    for copy in copies:
        copy.wait()


def shards(n_sub, n_col, perm, accum, rhs, depth_x, depth_y):
    bx, by, nz = perm.shape
    ex, ey = bx + 2 * PADX, by + 2 * PADY
    field = pltpu.VMEM((ex, ey, nz), jnp.float32)
    strips_x = pltpu.VMEM((2, 8, ey, nz), jnp.float32)
    strips_y = pltpu.VMEM((2, ex, 16, nz), jnp.float32)
    hbm = pl.BlockSpec(memory_space=pl.ANY)
    vmem = pl.BlockSpec(memory_space=pltpu.VMEM)
    copies = 24 + 4 + 8
    result = pl.pallas_call(
        functools.partial(kernel, n_sub, n_col, bx, by),
        out_shape=pltpu.VMEM((bx, by, nz), jnp.float32),
        in_specs=[hbm, hbm, hbm, vmem, vmem],
        out_specs=vmem,
        scratch_shapes=[
            pltpu.VMEM((2, ey, nz), jnp.int32),
            pltpu.VMEM((2, ex, 8, nz), jnp.int32),
            pltpu.VMEM((2, 2, by), jnp.int32),
            pltpu.VMEM((2, 2, bx), jnp.int32),
        ] + [field] * 8 + [strips_x] * 3 + [strips_y] * 3 + [
            pltpu.SemaphoreType.DMA((copies,)),
            pltpu.SemaphoreType.DMA((copies,)),
            pltpu.SemaphoreType.DMA((3, bx // CHUNK)),
        ],
        compiler_params=pltpu.CompilerParams(
            collective_id=0, has_side_effects=True, vmem_limit_bytes=56 * 1024 * 1024),
        cost_estimate=pl.CostEstimate(
            flops=120 * bx * by * nz, bytes_accessed=16 * bx * by * nz, transcendentals=0),
    )(perm, accum, rhs, depth_x, depth_y.T)
    return pl.pallas_call(
        store,
        out_shape=jax.ShapeDtypeStruct((bx, by, nz), jnp.float32),
        in_specs=[vmem], out_specs=hbm,
        scratch_shapes=[pltpu.SemaphoreType.DMA((8,))],
        compiler_params=pltpu.CompilerParams(vmem_limit_bytes=4 * 1024 * 1024),
    )(result)


def solution(mesh):
    placed = (
        P("sub", "col", None),
        P("sub", "col", None),
        P("sub", "col", None),
        P("sub", "col"),
        P("sub", "col"),
    )
    return jax.shard_map(
        functools.partial(shards, mesh.shape["sub"], mesh.shape["col"]),
        mesh=mesh, in_specs=placed, out_specs=P("sub", "col", None), check_vma=False
    )
```

```python
import functools

import jax
import jax.numpy as jnp
from jax import lax
from jax.experimental import pallas as pl
from jax.experimental.pallas import tpu as pltpu
from jax.sharding import PartitionSpec as P

OVL = 4
VERTICAL = 0.1
MESH = pl.DeviceIdType.MESH

PADX = 3
PADY = 8
DIRS = ((-1, 0), (1, 0), (0, -1), (0, 1), (-1, -1), (-1, 1), (1, -1), (1, 1))
CHUNK = 8


def recip(value):
    return pl.reciprocal(value, approx=True)


def harmonic(first, second):
    return first * second * recip(first + second)


def kernel(n_sub, n_col, bx, by, perm, accum, rhs, depth_x, depth_y, out,
           dx_ref, dy_ref, hx, hy, pm, w, r, b, fx, fy, fz, pr,
           xw, xb, xc, yw, yb, yc, ssem, rsem, lsem):
    nz = 128
    s = lax.axis_index("sub")
    k = lax.axis_index("col")
    ex, ey = bx + 2 * PADX, by + 2 * PADY
    c = pm
    n_a, n_q = bx // 8 - 1, by // 8 + 1
    x_end, y_end = PADX + bx, PADY + by

    def exists(d):
        ok = None
        for coord, step, count in ((s, d[0], n_sub), (k, d[1], n_col)):
            if step == -1:
                test = coord > 0
            elif step == 1:
                test = coord < count - 1
            else:
                continue
            ok = test if ok is None else ok & test
        return ok

    def device(d):
        return (s + d[0], k + d[1])

    own_x, own_y = pl.ds(PADX, bx), pl.ds(PADY, by)

    def local(n):
        here = pl.ds(n * CHUNK, CHUNK)
        there = pl.ds(PADX + n * CHUNK, CHUNK)
        return [pltpu.make_async_copy(src.at[here], dst.at[there, own_y, :], lsem.at[i, n])
                for i, (src, dst) in enumerate(((perm, pm), (accum, w), (rhs, r)))]

    for n in range(bx // CHUNK):
        for copy in local(n):
            copy.start()

    def each(count, body):
        def step(i, carry):
            body(i)
            return carry
        lax.fori_loop(0, count, step, 0)

    def fill(value, *refs):
        for ref in refs:
            for x0 in (0, x_end):
                ref[x0:x0 + PADX, :, :] = jnp.full((PADX, ey, nz), value, jnp.float32)

        def rows(i):
            for ref in refs:
                for y0 in (0, y_end):
                    ref[pl.ds(PADX + 8 * i, 8), y0:y0 + PADY, :] = jnp.full((8, PADY, nz), value, jnp.float32)
        each(bx // 8, rows)

    fill(1e-30, pm)
    fill(1.0, w)
    fill(0.0, r, pr)
    hx[...] = jnp.zeros(hx.shape, jnp.int32)
    hy[...] = jnp.zeros(hy.shape, jnp.int32)

    barrier = pltpu.get_barrier_semaphore()
    arrivals = jnp.int32(0)
    for d in DIRS:
        @pl.when(exists(d))
        def _(d=d):
            pl.semaphore_signal(barrier, inc=1, device_id=device(d), device_id_type=MESH)
        arrivals = arrivals + jnp.where(exists(d), 1, 0).astype(jnp.int32)
    pl.semaphore_wait(barrier, arrivals)

    counter = [0]

    def remote(src, dst, d):
        i = counter[0]
        counter[0] += 1
        return d, pltpu.make_async_remote_copy(
            src_ref=src, dst_ref=dst, send_sem=ssem.at[i], recv_sem=rsem.at[i],
            device_id=device(d), device_id_type=MESH)

    def start(copies):
        for d, copy in copies:
            pl.when(exists(d))(copy.start)

    def wait_recv(copies):
        for d, copy in copies:
            pl.when(exists((-d[0], -d[1])))(copy.wait_recv)

    def wait_send(copies):
        for d, copy in copies:
            pl.when(exists(d))(copy.wait_send)

    def halo(src, ox, oy, dst, d, width):
        def span(step, offset, extent, pad, thick):
            if step == 0:
                return pl.ds(offset, extent), pl.ds(pad, extent)
            if step == 1:
                return pl.ds(offset + extent - thick, thick), pl.ds(pad - thick, thick)
            return pl.ds(offset, thick), pl.ds(pad + extent, thick)

        sxs, dxs = span(d[0], ox, bx, PADX, width)
        sys_, dys = span(d[1], oy, by, PADY, width)
        return remote(src.at[sxs, sys_, :], dst.at[dxs, dys, :], d)

    halos = [halo(perm, 0, 0, pm, d, 3) for d in DIRS]
    halos += [halo(accum, 0, 0, w, d, 2) for d in DIRS]
    halos += [halo(rhs, 0, 0, r, d, 2) for d in DIRS]
    halos += [remote(depth_y, hy.at[0], (1, 0)), remote(depth_y, hy.at[1], (-1, 0)),
              remote(depth_x, hx.at[0], (0, 1)), remote(depth_x, hx.at[1], (0, -1))]
    start(halos)

    for ref in (xb, xc):
        ref[0, 6:8] = jnp.zeros((2, ey, nz), jnp.float32)
        ref[1, 0:2] = jnp.zeros((2, ey, nz), jnp.float32)

    def clear(i):
        for ref in (yw, yb, yc):
            for u in range(2):
                ref[u, pl.ds(i * 2, 2)] = jnp.zeros((2, 16, nz), jnp.float32)
    each(ex // 2, clear)

    dx_ref[...] = jnp.zeros(dx_ref.shape, jnp.int32)
    dy_ref[...] = jnp.zeros(dy_ref.shape, jnp.int32)
    for side in range(2):
        dx_ref[side, own_y, :] = jnp.broadcast_to(depth_x[side:side + 1, :], (nz, by)).T
        lanes = jnp.broadcast_to(depth_y[side:side + 1, :], (nz, bx)).T
        dy_ref[side, own_x] = jnp.broadcast_to(lanes[:, None, :], (bx, 8, nz))

    def at(ref, x, y0):
        return ref[x, pl.ds(y0, 8), :]

    def put(ref, x, y0, value):
        ref[x, pl.ds(y0, 8), :] = value

    def strip_x(t):
        return PADX - 2 + t * (bx - 4)

    def strip_y(u):
        return PADY - 4 + u * (by - 8)

    sublane = lax.broadcasted_iota(jnp.int32, (8, nz), 0)
    lane = lax.broadcasted_iota(jnp.int32, (8, nz), 1)

    def stencil(ref, x0, y0, rows, emit, following=None, lx=0, ly=0):
        before, centre = at(ref, x0 - lx - 1, y0 - ly), at(ref, x0 - lx, y0 - ly)
        face = at(fx, x0 - 1, y0)
        backs = []
        for i in range(rows):
            x = x0 + i
            after = at(ref, x - lx + 1, y0 - ly)
            total = face * before
            face = at(fx, x, y0)
            total = total + face * after
            low = at(fy, x, y0)
            total = total + low * at(ref, x - lx, y0 - ly - 1)
            back = pltpu.roll(low * centre, 7, 0)
            if following is None:
                total = total + at(fy, x, y0 + 1) * at(ref, x - lx, y0 - ly + 1)
            else:
                total = total + jnp.where(sublane == 7, following[i], back)
            up = at(fz, x, y0)
            total = total + up * pltpu.roll(centre, nz - 1, 1)
            total = total + pltpu.roll(up * centre, 1, 1)
            emit(i, total, centre)
            backs.append(back)
            before, centre = centre, after
        return backs

    def coefficients(x0, y0, rows, emit, following=None):
        before, centre = 2.0 * at(pm, x0 - 1, y0), 2.0 * at(pm, x0, y0)
        face = harmonic(before, centre)
        put(fx, x0 - 1, y0, face)
        lows = []
        for i in range(rows):
            x = x0 + i
            after = 2.0 * at(pm, x + 1, y0)
            faces = face
            face = harmonic(centre, after)
            put(fx, x, y0, face)
            faces = faces + face
            low = harmonic(2.0 * at(pm, x, y0 - 1), centre)
            put(fy, x, y0, low)
            if following is None:
                high = harmonic(centre, 2.0 * at(pm, x, y0 + 1))
            else:
                high = pltpu.roll(jnp.where(sublane == 0, following[i], low), 7, 0)
            faces = faces + low + high
            scale = jnp.where(lane < nz - 1, jnp.float32(VERTICAL), 0.0)
            up = scale * harmonic(centre, pltpu.roll(centre, nz - 1, 1))
            put(fz, x, y0, up)
            faces = faces + up + pltpu.roll(up, 1, 1)
            emit(i, recip(at(w, x, y0) + faces))
            lows.append(low)
            centre = after
        return lows

    def end_y(t, u):
        return jnp.where(t == 0, hy[0, pl.ds(u, 1), bx - 1:bx], hy[1, pl.ds(u, 1), 0:1])

    def end_x(u, t):
        return jnp.where(u == 0, hx[0, pl.ds(t, 1), by - 1:by], hx[1, pl.ds(t, 1), 0:1])

    def strips(x0, y0, t, u):
        found = []
        if t is not None:
            found.append((xw.at[t], xb.at[t], x0 - strip_x(t), y0))
        if u is not None:
            found.append((yw.at[u], yb.at[u], x0, y0 - strip_y(u)))
        return found

    def frame_first(x0, y0, rows, t, u):
        j = y0 - PADY + sublane
        in_y = (j >= 0) & (j < by)
        if t is not None:
            deep_x = dx_ref[t, pl.ds(y0, 8), :]
        if u is not None:
            m_y = jnp.where(u == 0, j, by - 1 - j)
        if t is not None and u is not None:
            corner_x = (m_y == -1) & (end_y(t, u) >= 1)
            corner_y = (m_y == -1) & (end_x(u, t) >= 1)

        def emit(n, inverse):
            x = x0 + n
            i = x - PADX
            source = at(r, x, y0)
            if t is None:
                member = in_y
            else:
                m = jnp.where(t == 0, i, bx - 1 - i)
                beyond = m < 0
                member = jnp.where(beyond, -1 - m, jnp.where(in_y, -1, 8)) < deep_x
                other = jnp.where(beyond, jnp.where(in_y, -1, 8), m) < deep_x
                if u is not None:
                    other = other | (corner_x & (m == -1))
                weight = jnp.where(other, inverse, 0.0)
                put(xw.at[t], x - strip_x(t), y0, weight)
                put(xb.at[t], x - strip_x(t), y0, weight * source)
            if u is not None:
                deep_y = dy_ref[u, x]
                inside = jnp.where((i >= 0) & (i < bx), 0, 8)
                member = member | (jnp.where(m_y < 0, -1 - m_y, 8) < deep_y)
                other = jnp.where(m_y < 0, inside - 1, m_y) < deep_y
                if t is not None:
                    other = other | (corner_y & (m == -1))
                weight = jnp.where(other, inverse, 0.0)
                put(yw.at[u], x, y0 - strip_y(u), weight)
                put(yb.at[u], x, y0 - strip_y(u), weight * source)
            weight = jnp.where(member, inverse, 0.0)
            put(w, x, y0, weight)
            put(b, x, y0, weight * source)
        coefficients(x0, y0, rows, emit)

    def frame_again(x0, y0, rows, t, u):
        def emit(n, total, centre):
            x = x0 + n
            total = at(r, x, y0) + total
            for weights, target, x1, y1 in [(w, b, x0, y0)] + strips(x0, y0, t, u):
                weight = at(weights, x1 + n, y1)
                put(target, x1 + n, y1, jnp.where(weight > 0.0, weight * total - centre, 0.0))
        stencil(pr, x0, y0, rows, emit)

    def row(a):
        return PADX + 4 + 8 * a

    def column(q):
        return PADY - 4 + 8 * q

    def frame(block):
        unroll = 5 if (n_q - 2) % 5 == 0 else 1

        def along_x(n):
            t, q = n // ((n_q - 2) // unroll), n % ((n_q - 2) // unroll)
            for v in range(unroll):
                block(PADX - 2 + t * (bx - 2), column(1 + q * unroll + v), 6, t, None)
        each(2 * ((n_q - 2) // unroll), along_x)

        def along_y(u):
            for a in range(n_a):
                block(row(a), column(u * (n_q - 1)), 8, None, u)
        each(2, along_y)

        def corner(n):
            t, u = n // 2, n % 2
            block(PADX - 2 + t * (bx - 2), column(u * (n_q - 1)), 6, t, u)
        each(4, corner)

    def chain(body, columns, *args):
        following = None
        for q in reversed(columns):
            following = body(*args, q, following)

    def second(x0, rows, q, following):
        y0 = column(q)

        def emit(i, total, centre):
            put(c, x0 + i, y0, centre + at(w, x0 + i, y0) * total)
        return stencil(b, x0, y0, rows, emit, following)

    def second_inner():
        each(n_a - 2, lambda a: chain(second, range(2, n_q - 2), row(a + 1), 8))

    def second_outer():
        def ends(a):
            chain(second, range(n_q - 2, n_q), row(a + 1), 8)
            chain(second, range(0, 2), row(a + 1), 8)
        each(n_a - 2, ends)
        each(2, lambda t: chain(second, range(n_q), PADX + 4 + t * (bx - 16), 8))
        each(2, lambda t: chain(second, range(n_q), PADX - 1 + t * (bx - 3), 5))

    def second_strips():
        def strip(src, dst, weight, x0, y0, rows, following, lx, ly):
            def emit(i, total, centre):
                x, y = x0 - lx + i, y0 - ly
                put(dst, x, y, centre + at(weight, x, y) * total)
            return stencil(src, x0, y0, rows, emit, following, lx, ly)

        def along_x(t):
            def block(q, following):
                return strip(xb.at[t], xc.at[t], xw.at[t], PADX - 1 + t * (bx - 3), column(q), 5, following, strip_x(t), 0)
            chain(block, range(n_q))
        each(2, along_x)

        def along_y(u):
            for a in range(bx // 8):
                strip(yb.at[u], yc.at[u], yw.at[u], PADX + 8 * a, PADY - 3 + u * (by - 2), 8, None, 0, strip_y(u))
        each(2, along_y)

    def finish(turn, x, y0, value):
        if turn == 0:
            put(pr, x, y0, value)
        else:
            put(out, x - PADX, y0 - PADY, at(pr, x, y0) + value)

    def third_inner(turn):
        def block(x0, q, following):
            y0 = PADY + 8 * q

            def emit(i, total, centre):
                x = x0 + i
                finish(turn, x, y0, at(b, x, y0) + at(w, x, y0) * total)
            return stencil(c, x0, y0, 8, emit, following)
        each(n_a, lambda a: chain(block, range(1, by // 8 - 1), row(a)))

    def border(turn, x0, y0, rows, t, u, following=(None, None)):
        sums, covers, backs = [None] * rows, [None] * rows, []

        def add(i, value, weight):
            sums[i] = value if sums[i] is None else sums[i] + value
            if weight is not None:
                covers[i] = jnp.where(weight > 0.0, 2.0 if covers[i] is None else covers[i] + 1.0,
                                      1.0 if covers[i] is None else covers[i])

        def own(i, total, centre):
            add(i, at(b, x0 + i, y0) + at(w, x0 + i, y0) * total, None)
        backs.append(stencil(c, x0, y0, rows, own, following[0]))
        for n, (weights, source, x1, y1) in enumerate(strips(x0, y0, t, u)):
            def other(i, total, centre, weights=weights, source=source, x1=x1, y1=y1):
                weight = at(weights, x1 + i, y1)
                add(i, at(source, x1 + i, y1) + weight * total, weight)
            along_x = t is not None and n == 0
            backs.append(stencil(xc.at[t] if along_x else yc.at[u], x0, y0, rows, other,
                                 following[1] if along_x else None, x0 - x1, y0 - y1))
        for i in range(rows):
            finish(turn, x0 + i, y0, sums[i] * recip(covers[i]))
        return backs

    def third_border(turn):
        def corner(n):
            t, u = n // 2, n % 2
            border(turn, PADX + t * (bx - 4), PADY + u * (by - 8), 4, t, u)
        each(4, corner)

        def along_x(t):
            following = (None, None)
            for q in reversed(range(1, by // 8 - 1)):
                following = border(turn, PADX + t * (bx - 4), PADY + 8 * q, 4, t, None, following)
        each(2, along_x)

        def along_y(u):
            for a in range(n_a):
                border(turn, row(a), PADY + u * (by - 8), 8, None, u)
        each(2, along_y)

    for copy in local(0):
        copy.wait()

    def first_row(a):
        for copy in local(a + 1):
            copy.wait()

        def block(x0, q, following):
            y0 = column(q)

            def emit(i, inverse):
                put(w, x0 + i, y0, inverse)
                put(b, x0 + i, y0, inverse * at(r, x0 + i, y0))
            return coefficients(x0, y0, 8, emit, following)
        chain(block, range(1, n_q - 1), row(a))
    each(n_a, first_row)
    second_inner()
    wait_recv(halos)
    frame(frame_first)
    second_outer()
    second_strips()
    third_border(0)
    spread = [halo(pr, PADX, PADY, pr, d, 3) for d in DIRS]
    start(spread)
    third_inner(0)

    def restart(x0, q, following):
        y0 = column(q)

        def emit(i, total, centre):
            x = x0 + i
            put(b, x, y0, at(w, x, y0) * (at(r, x, y0) + total) - centre)
        return stencil(pr, x0, y0, 8, emit, following)
    each(n_a, lambda a: chain(restart, range(1, n_q - 1), row(a)))
    second_inner()
    wait_recv(spread)
    frame(frame_again)
    second_outer()
    second_strips()
    third_border(1)
    third_inner(1)
    wait_send(halos)
    wait_send(spread)


def store(source, target, sem):
    rows = source.shape[0] // 8
    copies = [pltpu.make_async_copy(source.at[pl.ds(i * rows, rows)], target.at[pl.ds(i * rows, rows)], sem.at[i])
              for i in range(8)]
    for copy in copies:
        copy.start()
    for copy in copies:
        copy.wait()


def shards(n_sub, n_col, perm, accum, rhs, depth_x, depth_y):
    bx, by, nz = perm.shape
    ex, ey = bx + 2 * PADX, by + 2 * PADY
    field = pltpu.VMEM((ex, ey, nz), jnp.float32)
    strips_x = pltpu.VMEM((2, 8, ey, nz), jnp.float32)
    strips_y = pltpu.VMEM((2, ex, 16, nz), jnp.float32)
    hbm = pl.BlockSpec(memory_space=pl.ANY)
    vmem = pl.BlockSpec(memory_space=pltpu.VMEM)
    copies = 24 + 4 + 8
    result = pl.pallas_call(
        functools.partial(kernel, n_sub, n_col, bx, by),
        out_shape=pltpu.VMEM((bx, by, nz), jnp.float32),
        in_specs=[hbm, hbm, hbm, vmem, vmem],
        out_specs=vmem,
        scratch_shapes=[
            pltpu.VMEM((2, ey, nz), jnp.int32),
            pltpu.VMEM((2, ex, 8, nz), jnp.int32),
            pltpu.VMEM((2, 2, by), jnp.int32),
            pltpu.VMEM((2, 2, bx), jnp.int32),
        ] + [field] * 8 + [strips_x] * 3 + [strips_y] * 3 + [
            pltpu.SemaphoreType.DMA((copies,)),
            pltpu.SemaphoreType.DMA((copies,)),
            pltpu.SemaphoreType.DMA((3, bx // CHUNK)),
        ],
        compiler_params=pltpu.CompilerParams(
            collective_id=0, has_side_effects=True, vmem_limit_bytes=56 * 1024 * 1024),
        cost_estimate=pl.CostEstimate(
            flops=120 * bx * by * nz, bytes_accessed=16 * bx * by * nz, transcendentals=0),
    )(perm, accum, rhs, depth_x, depth_y.T)
    return pl.pallas_call(
        store,
        out_shape=jax.ShapeDtypeStruct((bx, by, nz), jnp.float32),
        in_specs=[vmem], out_specs=hbm,
        scratch_shapes=[pltpu.SemaphoreType.DMA((8,))],
        compiler_params=pltpu.CompilerParams(vmem_limit_bytes=4 * 1024 * 1024),
    )(result)


def solution(mesh):
    placed = (
        P("sub", "col", None),
        P("sub", "col", None),
        P("sub", "col", None),
        P("sub", "col"),
        P("sub", "col"),
    )
    return jax.shard_map(
        functools.partial(shards, mesh.shape["sub"], mesh.shape["col"]),
        mesh=mesh, in_specs=placed, out_specs=P("sub", "col", None), check_vma=False
    )
```

```python
import functools

import jax
import jax.numpy as jnp
from jax import lax
from jax.experimental import pallas as pl
from jax.experimental.pallas import tpu as pltpu
from jax.sharding import PartitionSpec as P

OVL = 4
VERTICAL = 0.1
MESH = pl.DeviceIdType.MESH

PADX = 3
PADY = 8
DIRS = ((-1, 0), (1, 0), (0, -1), (0, 1), (-1, -1), (-1, 1), (1, -1), (1, 1))
CHUNK = 8


def recip(value):
    return pl.reciprocal(value, approx=True)


def harmonic(first, second):
    return first * second * recip(first + second)


def kernel(n_sub, n_col, bx, by, perm, accum, rhs, depth_x, depth_y, out,
           dx_ref, dy_ref, kx, ky, hx, hy, pm, w, r, b, fx, fy, fz, pr,
           xw, xb, xc, yw, yb, yc, ssem, rsem, lsem, dsem):
    nz = 128
    s = lax.axis_index("sub")
    k = lax.axis_index("col")
    ex, ey = bx + 2 * PADX, by + 2 * PADY
    c = pm
    n_a, n_q = bx // 8 - 1, by // 8 + 1
    x_end, y_end = PADX + bx, PADY + by

    def exists(d):
        ok = None
        for coord, step, count in ((s, d[0], n_sub), (k, d[1], n_col)):
            if step == -1:
                test = coord > 0
            elif step == 1:
                test = coord < count - 1
            else:
                continue
            ok = test if ok is None else ok & test
        return ok

    def device(d):
        return (s + d[0], k + d[1])

    own_x, own_y = pl.ds(PADX, bx), pl.ds(PADY, by)

    def local(n):
        here = pl.ds(n * CHUNK, CHUNK)
        there = pl.ds(PADX + n * CHUNK, CHUNK)
        return [pltpu.make_async_copy(src.at[here], dst.at[there, own_y, :], lsem.at[i, n])
                for i, (src, dst) in enumerate(((perm, pm), (accum, w), (rhs, r)))]

    depths = [pltpu.make_async_copy(depth_x, kx, dsem.at[0]), pltpu.make_async_copy(depth_y, ky, dsem.at[1])]
    for n in range(bx // CHUNK):
        for copy in local(n):
            copy.start()
        if n == 0:
            for copy in depths:
                copy.start()

    def each(count, body, first=0):
        def step(i, carry):
            body(i)
            return carry
        lax.fori_loop(first, count, step, 0)

    def fill(value, *refs):
        for ref in refs:
            for x0 in (0, x_end):
                ref[x0:x0 + PADX, :, :] = jnp.full((PADX, ey, nz), value, jnp.float32)

        def rows(i):
            for ref in refs:
                for y0 in (0, y_end):
                    ref[pl.ds(PADX + 8 * i, 8), y0:y0 + PADY, :] = jnp.full((8, PADY, nz), value, jnp.float32)
        each(bx // 8, rows)

    fill(1e-30, pm)
    fill(1.0, w)
    fill(0.0, r, pr)
    hx[...] = jnp.zeros(hx.shape, jnp.int32)
    hy[...] = jnp.zeros(hy.shape, jnp.int32)

    barrier = pltpu.get_barrier_semaphore()
    arrivals = jnp.int32(0)
    for d in DIRS:
        @pl.when(exists(d))
        def _(d=d):
            pl.semaphore_signal(barrier, inc=1, device_id=device(d), device_id_type=MESH)
        arrivals = arrivals + jnp.where(exists(d), 1, 0).astype(jnp.int32)
    pl.semaphore_wait(barrier, arrivals)

    counter = [0]

    def remote(src, dst, d):
        i = counter[0]
        counter[0] += 1
        return d, pltpu.make_async_remote_copy(
            src_ref=src, dst_ref=dst, send_sem=ssem.at[i], recv_sem=rsem.at[i],
            device_id=device(d), device_id_type=MESH)

    def start(copies):
        for d, copy in copies:
            pl.when(exists(d))(copy.start)

    def wait_recv(copies):
        for d, copy in copies:
            pl.when(exists((-d[0], -d[1])))(copy.wait_recv)

    def wait_send(copies):
        for d, copy in copies:
            pl.when(exists(d))(copy.wait_send)

    def halo(src, ox, oy, dst, d, width):
        def span(step, offset, extent, pad, thick):
            if step == 0:
                return pl.ds(offset, extent), pl.ds(pad, extent)
            if step == 1:
                return pl.ds(offset + extent - thick, thick), pl.ds(pad - thick, thick)
            return pl.ds(offset, thick), pl.ds(pad + extent, thick)

        sxs, dxs = span(d[0], ox, bx, PADX, width)
        sys_, dys = span(d[1], oy, by, PADY, width)
        return remote(src.at[sxs, sys_, :], dst.at[dxs, dys, :], d)

    def given(d):
        return [halo(perm, 0, 0, pm, d, 3), halo(accum, 0, 0, w, d, 2), halo(rhs, 0, 0, r, d, 2)]

    halos_x = [copy for pair in zip(given(DIRS[0]), given(DIRS[1])) for copy in pair]
    halos_y = [copy for pair in zip(given(DIRS[2]), given(DIRS[3])) for copy in pair]
    halos_x += [remote(depth_y, hy.at[0], (1, 0)), remote(depth_y, hy.at[1], (-1, 0)),
                remote(depth_x, hx.at[0], (0, 1)), remote(depth_x, hx.at[1], (0, -1))]
    halos_x += [copy for d in DIRS[4:] for copy in given(d)]
    start(halos_y)
    start(halos_x)

    for ref in (xb, xc):
        ref[0, 6:8] = jnp.zeros((2, ey, nz), jnp.float32)
        ref[1, 0:2] = jnp.zeros((2, ey, nz), jnp.float32)

    def clear(i):
        for ref in (yw, yb, yc):
            for u in range(2):
                ref[u, pl.ds(i * 10, 10), 8 - 8 * u:16 - 8 * u] = jnp.zeros((10, 8, nz), jnp.float32)
    each(ex // 10, clear)
    for u in range(2):
        for x in (PADX - 1, x_end):
            yc[u, x] = jnp.zeros((16, nz), jnp.float32)

    for copy in depths:
        copy.wait()
    dx_ref[...] = jnp.zeros(dx_ref.shape, jnp.int32)
    dy_ref[...] = jnp.zeros(dy_ref.shape, jnp.int32)
    for side in range(2):
        dx_ref[side, own_y, :] = jnp.broadcast_to(kx[side:side + 1, :], (nz, by)).T
        lanes = jnp.broadcast_to(ky[side:side + 1, :], (nz, bx)).T
        dy_ref[side, own_x] = jnp.broadcast_to(lanes[:, None, :], (bx, 8, nz))

    def at(ref, x, y0):
        return ref[x, pl.ds(y0, 8), :]

    def put(ref, x, y0, value):
        ref[x, pl.ds(y0, 8), :] = value

    def strip_x(t):
        return PADX - 2 + t * (bx - 4)

    def strip_y(u):
        return PADY - 4 + u * (by - 8)

    sublane = lax.broadcasted_iota(jnp.int32, (8, nz), 0)
    lane = lax.broadcasted_iota(jnp.int32, (8, nz), 1)

    def stencil(ref, x0, y0, rows, emit, following=None, lx=0, ly=0):
        before, centre = at(ref, x0 - lx - 1, y0 - ly), at(ref, x0 - lx, y0 - ly)
        face = at(fx, x0 - 1, y0)
        backs = []
        for i in range(rows):
            x = x0 + i
            after = at(ref, x - lx + 1, y0 - ly)
            total = face * before
            face = at(fx, x, y0)
            total = total + face * after
            low = at(fy, x, y0)
            total = total + low * at(ref, x - lx, y0 - ly - 1)
            back = pltpu.roll(low * centre, 7, 0)
            if following is None:
                total = total + at(fy, x, y0 + 1) * at(ref, x - lx, y0 - ly + 1)
            else:
                total = total + jnp.where(sublane == 7, following[i], back)
            up = at(fz, x, y0)
            total = total + up * pltpu.roll(centre, nz - 1, 1)
            total = total + pltpu.roll(up * centre, 1, 1)
            emit(i, total, centre)
            backs.append(back)
            before, centre = centre, after
        return backs

    def coefficients(x0, y0, rows, emit, following=None):
        before, centre = 2.0 * at(pm, x0 - 1, y0), 2.0 * at(pm, x0, y0)
        face = harmonic(before, centre)
        put(fx, x0 - 1, y0, face)
        lows = []
        for i in range(rows):
            x = x0 + i
            after = 2.0 * at(pm, x + 1, y0)
            faces = face
            face = harmonic(centre, after)
            put(fx, x, y0, face)
            faces = faces + face
            low = harmonic(2.0 * at(pm, x, y0 - 1), centre)
            put(fy, x, y0, low)
            if following is None:
                high = harmonic(centre, 2.0 * at(pm, x, y0 + 1))
            else:
                high = pltpu.roll(jnp.where(sublane == 0, following[i], low), 7, 0)
            faces = faces + low + high
            scale = jnp.where(lane < nz - 1, jnp.float32(VERTICAL), 0.0)
            up = scale * harmonic(centre, pltpu.roll(centre, nz - 1, 1))
            put(fz, x, y0, up)
            faces = faces + up + pltpu.roll(up, 1, 1)
            emit(i, recip(at(w, x, y0) + faces))
            lows.append(low)
            centre = after
        return lows

    def end_y(t, u):
        return jnp.where(t == 0, hy[0, pl.ds(u, 1), bx - 1:bx], hy[1, pl.ds(u, 1), 0:1])

    def end_x(u, t):
        return jnp.where(u == 0, hx[0, pl.ds(t, 1), by - 1:by], hx[1, pl.ds(t, 1), 0:1])

    def strips(x0, y0, t, u):
        found = []
        if t is not None:
            found.append((xw.at[t], xb.at[t], x0 - strip_x(t), y0))
        if u is not None:
            found.append((yw.at[u], yb.at[u], x0, y0 - strip_y(u)))
        return found

    def frame_first(x0, y0, rows, t, u):
        j = y0 - PADY + sublane
        in_y = (j >= 0) & (j < by)
        if t is not None:
            deep_x = dx_ref[t, pl.ds(y0, 8), :]
        if u is not None:
            m_y = jnp.where(u == 0, j, by - 1 - j)
        if t is not None and u is not None:
            corner_x = (m_y == -1) & (end_y(t, u) >= 1)
            corner_y = (m_y == -1) & (end_x(u, t) >= 1)

        def emit(n, inverse):
            x = x0 + n
            i = x - PADX
            source = at(r, x, y0)
            if t is None:
                member = in_y
            else:
                m = jnp.where(t == 0, i, bx - 1 - i)
                beyond = m < 0
                member = jnp.where(beyond, -1 - m, jnp.where(in_y, -1, 8)) < deep_x
                other = jnp.where(beyond, jnp.where(in_y, -1, 8), m) < deep_x
                if u is not None:
                    other = other | (corner_x & (m == -1))
                weight = jnp.where(other, inverse, 0.0)
                put(xw.at[t], x - strip_x(t), y0, weight)
                put(xb.at[t], x - strip_x(t), y0, weight * source)
            if u is not None:
                deep_y = dy_ref[u, x]
                inside = jnp.where((i >= 0) & (i < bx), 0, 8)
                member = member | (jnp.where(m_y < 0, -1 - m_y, 8) < deep_y)
                other = jnp.where(m_y < 0, inside - 1, m_y) < deep_y
                if t is not None:
                    other = other | (corner_y & (m == -1))
                weight = jnp.where(other, inverse, 0.0)
                put(yw.at[u], x, y0 - strip_y(u), weight)
                put(yb.at[u], x, y0 - strip_y(u), weight * source)
            weight = jnp.where(member, inverse, 0.0)
            put(w, x, y0, weight)
            put(b, x, y0, weight * source)
        coefficients(x0, y0, rows, emit)

    def frame_again(x0, y0, rows, t, u):
        def emit(n, total, centre):
            x = x0 + n
            total = at(r, x, y0) + total
            for weights, target, x1, y1 in [(w, b, x0, y0)] + strips(x0, y0, t, u):
                weight = at(weights, x1 + n, y1)
                put(target, x1 + n, y1, jnp.where(weight > 0.0, weight * total - centre, 0.0))
        stencil(pr, x0, y0, rows, emit)

    def row(a):
        return PADX + 4 + 8 * a

    def column(q):
        return PADY - 4 + 8 * q

    def frame_x(block):
        unroll = 5 if (n_q - 2) % 5 == 0 else 1

        def along_x(n):
            t, q = n // ((n_q - 2) // unroll), n % ((n_q - 2) // unroll)
            for v in range(unroll):
                block(PADX - 2 + t * (bx - 2), column(1 + q * unroll + v), 6, t, None)
        each(2 * ((n_q - 2) // unroll), along_x)

        def corner(n):
            t, u = n // 2, n % 2
            block(PADX - 2 + t * (bx - 2), column(u * (n_q - 1)), 6, t, u)
        each(4, corner)

    def frame_y(block):
        def along_y(u):
            for a in range(n_a):
                block(row(a), column(u * (n_q - 1)), 8, None, u)
        each(2, along_y)

    def chain(body, columns, *args):
        following = None
        for q in reversed(columns):
            following = body(*args, q, following)

    def second(x0, rows, q, following):
        y0 = column(q)

        def emit(i, total, centre):
            put(c, x0 + i, y0, centre + at(w, x0 + i, y0) * total)
        return stencil(b, x0, y0, rows, emit, following)

    def second_inner():
        each(n_a - 2, lambda a: chain(second, range(2, n_q - 2), row(a + 1), 8))

    def second_ends():
        def ends(a):
            chain(second, range(n_q - 2, n_q), row(a + 1), 8)
            chain(second, range(0, 2), row(a + 1), 8)
        each(n_a - 2, ends)

    def second_rows():
        each(2, lambda t: chain(second, range(n_q), PADX + 4 + t * (bx - 16), 8))
        each(2, lambda t: chain(second, range(n_q), PADX - 1 + t * (bx - 3), 5))

    def strip(src, dst, weight, x0, y0, rows, following, lx, ly):
        def emit(i, total, centre):
            x, y = x0 - lx + i, y0 - ly
            put(dst, x, y, centre + at(weight, x, y) * total)
        return stencil(src, x0, y0, rows, emit, following, lx, ly)

    def strips_along_x():
        def along_x(t):
            def block(q, following):
                return strip(xb.at[t], xc.at[t], xw.at[t], PADX - 1 + t * (bx - 3), column(q), 5, following, strip_x(t), 0)
            chain(block, range(n_q))
        each(2, along_x)

    def strips_along_y(*rows):
        def along_y(u):
            for a in rows:
                strip(yb.at[u], yc.at[u], yw.at[u], PADX + 8 * a, PADY - 3 + u * (by - 2), 8, None, 0, strip_y(u))
        each(2, along_y)

    def finish(turn, x, y0, value):
        if turn == 0:
            put(pr, x, y0, value)
        else:
            put(out, x - PADX, y0 - PADY, at(pr, x, y0) + value)

    def third_inner(turn):
        def block(x0, q, following):
            y0 = PADY + 8 * q

            def emit(i, total, centre):
                x = x0 + i
                finish(turn, x, y0, at(b, x, y0) + at(w, x, y0) * total)
            return stencil(c, x0, y0, 8, emit, following)
        return lambda a: chain(block, range(1, by // 8 - 1), row(a))

    def border(turn, x0, y0, rows, t, u, following=(None, None)):
        sums, covers, backs = [None] * rows, [None] * rows, []

        def add(i, value, weight):
            sums[i] = value if sums[i] is None else sums[i] + value
            if weight is not None:
                covers[i] = jnp.where(weight > 0.0, 2.0 if covers[i] is None else covers[i] + 1.0,
                                      1.0 if covers[i] is None else covers[i])

        def own(i, total, centre):
            add(i, at(b, x0 + i, y0) + at(w, x0 + i, y0) * total, None)
        backs.append(stencil(c, x0, y0, rows, own, following[0]))
        for n, (weights, source, x1, y1) in enumerate(strips(x0, y0, t, u)):
            def other(i, total, centre, weights=weights, source=source, x1=x1, y1=y1):
                weight = at(weights, x1 + i, y1)
                add(i, at(source, x1 + i, y1) + weight * total, weight)
            along_x = t is not None and n == 0
            backs.append(stencil(xc.at[t] if along_x else yc.at[u], x0, y0, rows, other,
                                 following[1] if along_x else None, x0 - x1, y0 - y1))
        for i in range(rows):
            finish(turn, x0 + i, y0, sums[i] * recip(covers[i]))
        return backs

    def border_x(turn):
        def corner(n):
            t, u = n // 2, n % 2
            border(turn, PADX + t * (bx - 4), PADY + u * (by - 8), 4, t, u)
        each(4, corner)

        def along_x(t):
            following = (None, None)
            for q in reversed(range(1, by // 8 - 1)):
                following = border(turn, PADX + t * (bx - 4), PADY + 8 * q, 4, t, None, following)
        each(2, along_x)

    def border_y(turn, *rows):
        def along_y(u):
            for a in rows:
                border(turn, row(a), PADY + u * (by - 8), 8, None, u)
        each(2, along_y)

    for copy in local(0):
        copy.wait()

    def first_row(a):
        for copy in local(a + 1):
            copy.wait()

        def block(x0, q, following):
            y0 = column(q)

            def emit(i, inverse):
                put(w, x0 + i, y0, inverse)
                put(b, x0 + i, y0, inverse * at(r, x0 + i, y0))
            return coefficients(x0, y0, 8, emit, following)
        chain(block, range(1, n_q - 1), row(a))
    each(n_a, first_row)
    middle = range(2, n_a - 2)
    ends = [a for a in range(n_a) if a not in middle]

    def correct(turn, frame, along_y, along_x):
        second_inner()
        wait_recv(along_y)
        frame_y(frame)
        second_ends()
        strips_along_y(*range(1, bx // 8 - 1))
        border_y(turn, *middle)
        each(n_a - 2, third_inner(turn), 2)
        wait_recv(along_x)
        frame_x(frame)
        second_rows()
        strips_along_x()
        strips_along_y(0, bx // 8 - 1)
        border_x(turn)
        border_y(turn, *ends)

    def third_ends(turn):
        each(4, lambda n: third_inner(turn)(n + (n // 2) * (n_a - 4)))

    correct(0, frame_first, halos_y, halos_x)
    spread = [halo(pr, PADX, PADY, pr, d, 3) for d in (*DIRS[2:4], *DIRS[0:2], *DIRS[4:])]
    start(spread)
    third_ends(0)

    def restart(x0, q, following):
        y0 = column(q)

        def emit(i, total, centre):
            x = x0 + i
            put(b, x, y0, at(w, x, y0) * (at(r, x, y0) + total) - centre)
        return stencil(pr, x0, y0, 8, emit, following)
    each(n_a, lambda a: chain(restart, range(1, n_q - 1), row(a)))
    correct(1, frame_again, spread[:2], spread[2:])
    third_ends(1)
    wait_send(halos_y)
    wait_send(halos_x)
    wait_send(spread)


def store(source, target, sem):
    rows = source.shape[0] // 8
    copies = [pltpu.make_async_copy(source.at[pl.ds(i * rows, rows)], target.at[pl.ds(i * rows, rows)], sem.at[i])
              for i in range(8)]
    for copy in copies:
        copy.start()
    for copy in copies:
        copy.wait()


def shards(n_sub, n_col, perm, accum, rhs, depth_x, depth_y):
    bx, by, nz = perm.shape
    ex, ey = bx + 2 * PADX, by + 2 * PADY
    field = pltpu.VMEM((ex, ey, nz), jnp.float32)
    strips_x = pltpu.VMEM((2, 8, ey, nz), jnp.float32)
    strips_y = pltpu.VMEM((2, ex, 16, nz), jnp.float32)
    hbm = pl.BlockSpec(memory_space=pl.ANY)
    vmem = pl.BlockSpec(memory_space=pltpu.VMEM)
    copies = 24 + 4 + 8
    result = pl.pallas_call(
        functools.partial(kernel, n_sub, n_col, bx, by),
        out_shape=pltpu.VMEM((bx, by, nz), jnp.float32),
        in_specs=[hbm] * 5,
        out_specs=vmem,
        scratch_shapes=[
            pltpu.VMEM((2, ey, nz), jnp.int32),
            pltpu.VMEM((2, ex, 8, nz), jnp.int32),
            pltpu.VMEM((2, by), jnp.int32),
            pltpu.VMEM((2, bx), jnp.int32),
            pltpu.VMEM((2, 2, by), jnp.int32),
            pltpu.VMEM((2, 2, bx), jnp.int32),
        ] + [field] * 8 + [strips_x] * 3 + [strips_y] * 3 + [
            pltpu.SemaphoreType.DMA((copies,)),
            pltpu.SemaphoreType.DMA((copies,)),
            pltpu.SemaphoreType.DMA((3, bx // CHUNK)),
            pltpu.SemaphoreType.DMA((2,)),
        ],
        compiler_params=pltpu.CompilerParams(
            collective_id=0, has_side_effects=True, vmem_limit_bytes=56 * 1024 * 1024),
        cost_estimate=pl.CostEstimate(
            flops=120 * bx * by * nz, bytes_accessed=16 * bx * by * nz, transcendentals=0),
    )(perm, accum, rhs, depth_x, depth_y.T)
    return pl.pallas_call(
        store,
        out_shape=jax.ShapeDtypeStruct((bx, by, nz), jnp.float32),
        in_specs=[vmem], out_specs=hbm,
        scratch_shapes=[pltpu.SemaphoreType.DMA((8,))],
        compiler_params=pltpu.CompilerParams(vmem_limit_bytes=4 * 1024 * 1024),
    )(result)


def solution(mesh):
    placed = (
        P("sub", "col", None),
        P("sub", "col", None),
        P("sub", "col", None),
        P("sub", "col"),
        P("sub", "col"),
    )
    return jax.shard_map(
        functools.partial(shards, mesh.shape["sub"], mesh.shape["col"]),
        mesh=mesh, in_specs=placed, out_specs=P("sub", "col", None), check_vma=False
    )
```

```python
import functools

import jax
import jax.numpy as jnp
from jax import lax
from jax.experimental import pallas as pl
from jax.experimental.pallas import tpu as pltpu
from jax.sharding import PartitionSpec as P

OVL = 4
VERTICAL = 0.1
MESH = pl.DeviceIdType.MESH

PADX = 3
PADY = 8
DIRS = ((-1, 0), (1, 0), (0, -1), (0, 1), (-1, -1), (-1, 1), (1, -1), (1, 1))
CHUNK = 8


def recip(value):
    return pl.reciprocal(value, approx=True)


def harmonic(first, second):
    return first * second * recip(first + second)


def kernel(n_sub, n_col, bx, by, perm, accum, rhs, depth_x, depth_y, out,
           dx_ref, dy_ref, kx, ky, hx, hy, pm, w, r, b, fx, fy, fz, pr,
           xw, xb, xc, yw, yb, yc, ssem, rsem, lsem, dsem):
    nz = 128
    s = lax.axis_index("sub")
    k = lax.axis_index("col")
    ex, ey = bx + 2 * PADX, by + 2 * PADY
    c = pm
    n_a, n_q = bx // 8 - 1, by // 8 + 1
    x_end, y_end = PADX + bx, PADY + by

    def exists(d):
        ok = None
        for coord, step, count in ((s, d[0], n_sub), (k, d[1], n_col)):
            if step == -1:
                test = coord > 0
            elif step == 1:
                test = coord < count - 1
            else:
                continue
            ok = test if ok is None else ok & test
        return ok

    def device(d):
        return (s + d[0], k + d[1])

    own_x, own_y = pl.ds(PADX, bx), pl.ds(PADY, by)

    def local(n):
        here = pl.ds(n * CHUNK, CHUNK)
        there = pl.ds(PADX + n * CHUNK, CHUNK)
        return [pltpu.make_async_copy(src.at[here], dst.at[there, own_y, :], lsem.at[i, n])
                for i, (src, dst) in enumerate(((perm, pm), (accum, w), (rhs, r)))]

    depths = [pltpu.make_async_copy(depth_x, kx, dsem.at[0]), pltpu.make_async_copy(depth_y, ky, dsem.at[1])]
    for n in range(bx // CHUNK):
        for copy in local(n):
            copy.start()
        if n == 0:
            for copy in depths:
                copy.start()

    def each(count, body, first=0):
        def step(i, carry):
            body(i)
            return carry
        lax.fori_loop(first, count, step, 0)

    def fill(value, *refs):
        for ref in refs:
            for x0 in (0, x_end):
                ref[x0:x0 + PADX, :, :] = jnp.full((PADX, ey, nz), value, jnp.float32)

        def rows(i):
            for ref in refs:
                for y0 in (0, y_end):
                    ref[pl.ds(PADX + 8 * i, 8), y0:y0 + PADY, :] = jnp.full((8, PADY, nz), value, jnp.float32)
        each(bx // 8, rows)

    fill(1e-30, pm)
    fill(1.0, w)
    fill(0.0, r, pr)
    hx[...] = jnp.zeros(hx.shape, jnp.int32)
    hy[...] = jnp.zeros(hy.shape, jnp.int32)

    barrier = pltpu.get_barrier_semaphore()
    arrivals = jnp.int32(0)
    for d in DIRS:
        @pl.when(exists(d))
        def _(d=d):
            pl.semaphore_signal(barrier, inc=1, device_id=device(d), device_id_type=MESH)
        arrivals = arrivals + jnp.where(exists(d), 1, 0).astype(jnp.int32)
    counter = [0]

    def remote(src, dst, d):
        i = counter[0]
        counter[0] += 1
        return d, pltpu.make_async_remote_copy(
            src_ref=src, dst_ref=dst, send_sem=ssem.at[i], recv_sem=rsem.at[i],
            device_id=device(d), device_id_type=MESH)

    def start(copies):
        for d, copy in copies:
            pl.when(exists(d))(copy.start)

    def wait_recv(copies):
        for d, copy in copies:
            pl.when(exists((-d[0], -d[1])))(copy.wait_recv)

    def wait_send(copies):
        for d, copy in copies:
            pl.when(exists(d))(copy.wait_send)

    def halo(src, ox, oy, dst, d, width):
        def span(step, offset, extent, pad, thick):
            if step == 0:
                return pl.ds(offset, extent), pl.ds(pad, extent)
            if step == 1:
                return pl.ds(offset + extent - thick, thick), pl.ds(pad - thick, thick)
            return pl.ds(offset, thick), pl.ds(pad + extent, thick)

        sxs, dxs = span(d[0], ox, bx, PADX, width)
        sys_, dys = span(d[1], oy, by, PADY, width)
        return remote(src.at[sxs, sys_, :], dst.at[dxs, dys, :], d)

    def given(d):
        return [halo(perm, 0, 0, pm, d, 3), halo(accum, 0, 0, w, d, 2), halo(rhs, 0, 0, r, d, 2)]

    halos_x = [copy for pair in zip(given(DIRS[0]), given(DIRS[1])) for copy in pair]
    halos_y = [copy for pair in zip(given(DIRS[2]), given(DIRS[3])) for copy in pair]
    halos_x += [remote(depth_y, hy.at[0], (1, 0)), remote(depth_y, hy.at[1], (-1, 0)),
                remote(depth_x, hx.at[0], (0, 1)), remote(depth_x, hx.at[1], (0, -1))]
    halos_x += [copy for d in DIRS[4:] for copy in given(d)]

    def greet():
        pl.semaphore_wait(barrier, arrivals)
        start(halos_y)
        start(halos_x)

    for ref in (xb, xc):
        ref[0, 6:8] = jnp.zeros((2, ey, nz), jnp.float32)
        ref[1, 0:2] = jnp.zeros((2, ey, nz), jnp.float32)

    def clear(i):
        for ref in (yw, yb, yc):
            for u in range(2):
                ref[u, pl.ds(i * 10, 10), 8 - 8 * u:16 - 8 * u] = jnp.zeros((10, 8, nz), jnp.float32)
    each(ex // 10, clear)
    for u in range(2):
        for x in (PADX - 1, x_end):
            yc[u, x] = jnp.zeros((16, nz), jnp.float32)

    for copy in depths:
        copy.wait()
    dx_ref[...] = jnp.zeros(dx_ref.shape, jnp.int32)
    dy_ref[...] = jnp.zeros(dy_ref.shape, jnp.int32)
    for side in range(2):
        dx_ref[side, own_y, :] = jnp.broadcast_to(kx[side:side + 1, :], (nz, by)).T
        lanes = jnp.broadcast_to(ky[side:side + 1, :], (nz, bx)).T
        dy_ref[side, own_x] = jnp.broadcast_to(lanes[:, None, :], (bx, 8, nz))

    def at(ref, x, y0):
        return ref[x, pl.ds(y0, 8), :]

    def put(ref, x, y0, value):
        ref[x, pl.ds(y0, 8), :] = value

    def strip_x(t):
        return PADX - 2 + t * (bx - 4)

    def strip_y(u):
        return PADY - 4 + u * (by - 8)

    sublane = lax.broadcasted_iota(jnp.int32, (8, nz), 0)
    lane = lax.broadcasted_iota(jnp.int32, (8, nz), 1)

    def stencil(ref, x0, y0, rows, emit, following=None, lx=0, ly=0):
        before, centre = at(ref, x0 - lx - 1, y0 - ly), at(ref, x0 - lx, y0 - ly)
        face = at(fx, x0 - 1, y0)
        backs = []
        for i in range(rows):
            x = x0 + i
            after = at(ref, x - lx + 1, y0 - ly)
            total = face * before
            face = at(fx, x, y0)
            total = total + face * after
            low = at(fy, x, y0)
            total = total + low * at(ref, x - lx, y0 - ly - 1)
            back = pltpu.roll(low * centre, 7, 0)
            if following is None:
                total = total + at(fy, x, y0 + 1) * at(ref, x - lx, y0 - ly + 1)
            else:
                total = total + jnp.where(sublane == 7, following[i], back)
            up = at(fz, x, y0)
            total = total + up * pltpu.roll(centre, nz - 1, 1)
            total = total + pltpu.roll(up * centre, 1, 1)
            emit(i, total, centre)
            backs.append(back)
            before, centre = centre, after
        return backs

    def coefficients(x0, y0, rows, emit, following=None):
        before, centre = 2.0 * at(pm, x0 - 1, y0), 2.0 * at(pm, x0, y0)
        face = harmonic(before, centre)
        put(fx, x0 - 1, y0, face)
        lows = []
        for i in range(rows):
            x = x0 + i
            after = 2.0 * at(pm, x + 1, y0)
            faces = face
            face = harmonic(centre, after)
            put(fx, x, y0, face)
            faces = faces + face
            low = harmonic(2.0 * at(pm, x, y0 - 1), centre)
            put(fy, x, y0, low)
            if following is None:
                high = harmonic(centre, 2.0 * at(pm, x, y0 + 1))
            else:
                high = pltpu.roll(jnp.where(sublane == 0, following[i], low), 7, 0)
            faces = faces + low + high
            scale = jnp.where(lane < nz - 1, jnp.float32(VERTICAL), 0.0)
            up = scale * harmonic(centre, pltpu.roll(centre, nz - 1, 1))
            put(fz, x, y0, up)
            faces = faces + up + pltpu.roll(up, 1, 1)
            emit(i, recip(at(w, x, y0) + faces))
            lows.append(low)
            centre = after
        return lows

    def end_y(t, u):
        return jnp.where(t == 0, hy[0, pl.ds(u, 1), bx - 1:bx], hy[1, pl.ds(u, 1), 0:1])

    def end_x(u, t):
        return jnp.where(u == 0, hx[0, pl.ds(t, 1), by - 1:by], hx[1, pl.ds(t, 1), 0:1])

    def strips(x0, y0, t, u):
        found = []
        if t is not None:
            found.append((xw.at[t], xb.at[t], x0 - strip_x(t), y0))
        if u is not None:
            found.append((yw.at[u], yb.at[u], x0, y0 - strip_y(u)))
        return found

    def frame_first(x0, y0, rows, t, u):
        j = y0 - PADY + sublane
        in_y = (j >= 0) & (j < by)
        if t is not None:
            deep_x = dx_ref[t, pl.ds(y0, 8), :]
        if u is not None:
            m_y = jnp.where(u == 0, j, by - 1 - j)
        if t is not None and u is not None:
            corner_x = (m_y == -1) & (end_y(t, u) >= 1)
            corner_y = (m_y == -1) & (end_x(u, t) >= 1)

        def emit(n, inverse):
            x = x0 + n
            i = x - PADX
            source = at(r, x, y0)
            if t is None:
                member = in_y
            else:
                m = jnp.where(t == 0, i, bx - 1 - i)
                beyond = m < 0
                member = jnp.where(beyond, -1 - m, jnp.where(in_y, -1, 8)) < deep_x
                other = jnp.where(beyond, jnp.where(in_y, -1, 8), m) < deep_x
                if u is not None:
                    other = other | (corner_x & (m == -1))
                weight = jnp.where(other, inverse, 0.0)
                put(xw.at[t], x - strip_x(t), y0, weight)
                put(xb.at[t], x - strip_x(t), y0, weight * source)
            if u is not None:
                deep_y = dy_ref[u, x]
                inside = jnp.where((i >= 0) & (i < bx), 0, 8)
                member = member | (jnp.where(m_y < 0, -1 - m_y, 8) < deep_y)
                other = jnp.where(m_y < 0, inside - 1, m_y) < deep_y
                if t is not None:
                    other = other | (corner_y & (m == -1))
                weight = jnp.where(other, inverse, 0.0)
                put(yw.at[u], x, y0 - strip_y(u), weight)
                put(yb.at[u], x, y0 - strip_y(u), weight * source)
            weight = jnp.where(member, inverse, 0.0)
            put(w, x, y0, weight)
            put(b, x, y0, weight * source)
        coefficients(x0, y0, rows, emit)

    def frame_again(x0, y0, rows, t, u):
        def emit(n, total, centre):
            x = x0 + n
            total = at(r, x, y0) + total
            for weights, target, x1, y1 in [(w, b, x0, y0)] + strips(x0, y0, t, u):
                weight = at(weights, x1 + n, y1)
                put(target, x1 + n, y1, jnp.where(weight > 0.0, weight * total - centre, 0.0))
        stencil(pr, x0, y0, rows, emit)

    def row(a):
        return PADX + 4 + 8 * a

    def column(q):
        return PADY - 4 + 8 * q

    def frame_x(block):
        unroll = 5 if (n_q - 2) % 5 == 0 else 1

        def along_x(n):
            t, q = n // ((n_q - 2) // unroll), n % ((n_q - 2) // unroll)
            for v in range(unroll):
                block(PADX - 2 + t * (bx - 2), column(1 + q * unroll + v), 6, t, None)
        each(2 * ((n_q - 2) // unroll), along_x)

        def corner(n):
            t, u = n // 2, n % 2
            block(PADX - 2 + t * (bx - 2), column(u * (n_q - 1)), 6, t, u)
        each(4, corner)

    def frame_y(block):
        def along_y(u):
            for a in range(n_a):
                block(row(a), column(u * (n_q - 1)), 8, None, u)
        each(2, along_y)

    def chain(body, columns, *args):
        following = None
        for q in reversed(columns):
            following = body(*args, q, following)

    def second(x0, rows, q, following):
        y0 = column(q)

        def emit(i, total, centre):
            put(c, x0 + i, y0, centre + at(w, x0 + i, y0) * total)
        return stencil(b, x0, y0, rows, emit, following)

    def second_row(a):
        chain(second, range(2, n_q - 2), row(a), 8)

    def second_ends():
        def ends(a):
            chain(second, range(n_q - 2, n_q), row(a + 1), 8)
            chain(second, range(0, 2), row(a + 1), 8)
        each(n_a - 2, ends)

    def second_rows():
        each(2, lambda t: chain(second, range(n_q), PADX + 4 + t * (bx - 16), 8))
        each(2, lambda t: chain(second, range(n_q), PADX - 1 + t * (bx - 3), 5))

    def strip(src, dst, weight, x0, y0, rows, following, lx, ly):
        def emit(i, total, centre):
            x, y = x0 - lx + i, y0 - ly
            put(dst, x, y, centre + at(weight, x, y) * total)
        return stencil(src, x0, y0, rows, emit, following, lx, ly)

    def strips_along_x():
        def along_x(t):
            def block(q, following):
                return strip(xb.at[t], xc.at[t], xw.at[t], PADX - 1 + t * (bx - 3), column(q), 5, following, strip_x(t), 0)
            chain(block, range(n_q))
        each(2, along_x)

    def strips_along_y(*rows):
        def along_y(u):
            for a in rows:
                strip(yb.at[u], yc.at[u], yw.at[u], PADX + 8 * a, PADY - 3 + u * (by - 2), 8, None, 0, strip_y(u))
        each(2, along_y)

    def finish(turn, x, y0, value):
        if turn == 0:
            put(pr, x, y0, value)
        else:
            put(out, x - PADX, y0 - PADY, at(pr, x, y0) + value)

    def third_rows(turn, x0, rows):
        def block(q, following):
            y0 = PADY + 8 * q

            def emit(i, total, centre):
                x = x0 + i
                finish(turn, x, y0, at(b, x, y0) + at(w, x, y0) * total)
            return stencil(c, x0, y0, rows, emit, following)
        chain(block, range(1, by // 8 - 1))

    def border(turn, x0, y0, rows, t, u, following=(None, None)):
        sums, covers, backs = [None] * rows, [None] * rows, []

        def add(i, value, weight):
            sums[i] = value if sums[i] is None else sums[i] + value
            if weight is not None:
                covers[i] = jnp.where(weight > 0.0, 2.0 if covers[i] is None else covers[i] + 1.0,
                                      1.0 if covers[i] is None else covers[i])

        def own(i, total, centre):
            add(i, at(b, x0 + i, y0) + at(w, x0 + i, y0) * total, None)
        backs.append(stencil(c, x0, y0, rows, own, following[0]))
        for n, (weights, source, x1, y1) in enumerate(strips(x0, y0, t, u)):
            def other(i, total, centre, weights=weights, source=source, x1=x1, y1=y1):
                weight = at(weights, x1 + i, y1)
                add(i, at(source, x1 + i, y1) + weight * total, weight)
            along_x = t is not None and n == 0
            backs.append(stencil(xc.at[t] if along_x else yc.at[u], x0, y0, rows, other,
                                 following[1] if along_x else None, x0 - x1, y0 - y1))
        for i in range(rows):
            finish(turn, x0 + i, y0, sums[i] * recip(covers[i]))
        return backs

    def border_x(turn):
        def corner(n):
            t, u = n // 2, n % 2
            border(turn, PADX + t * (bx - 4), PADY + u * (by - 8), 4, t, u)
        each(4, corner)

        def along_x(t):
            following = (None, None)
            for q in reversed(range(1, by // 8 - 1)):
                following = border(turn, PADX + t * (bx - 4), PADY + 8 * q, 4, t, None, following)
        each(2, along_x)

    def border_y(turn, *spans):
        def along_y(u):
            for x0, rows in spans:
                border(turn, x0, PADY + u * (by - 8), rows, None, u)
        each(2, along_y)

    for copy in local(0):
        copy.wait()

    def first_row(a):
        for copy in local(a + 1):
            copy.wait()
        pl.when(a == n_a // 2)(greet)

        def block(x0, q, following):
            y0 = column(q)

            def emit(i, inverse):
                put(w, x0 + i, y0, inverse)
                put(b, x0 + i, y0, inverse * at(r, x0 + i, y0))
            return coefficients(x0, y0, 8, emit, following)
        chain(block, range(1, n_q - 1), row(a))
    each(n_a, first_row)
    edge = 14
    part = (bx - 2 * edge) // 4

    def restart(x0, rows, q, following):
        y0 = column(q)

        def emit(i, total, centre):
            x = x0 + i
            put(b, x, y0, at(w, x, y0) * (at(r, x, y0) + total) - centre)
        return stencil(pr, x0, y0, rows, emit, following)

    def correct_middle(turn, frame):
        frame_y(frame)
        second_ends()
        strips_along_y(*range(1, bx // 8 - 1))
        border_y(turn, *[(PADX + edge + part * n, part) for n in range(4)])
        each(4, lambda n: third_rows(turn, PADX + edge + part * n, part))

    def correct_border(turn, frame):
        frame_x(frame)
        second_rows()
        strips_along_x()
        strips_along_y(0, bx // 8 - 1)
        border_x(turn)
        border_y(turn, (PADX + 4, edge - 4), (PADX + bx - edge, edge - 4))

    def third_ends(turn):
        each(2, lambda t: third_rows(turn, PADX + 4 + t * (bx - 4 - edge), edge - 4))

    each(n_a - 1, second_row, 1)
    wait_recv(halos_y)
    correct_middle(0, frame_first)
    early = 16
    each((bx - 2 * early) // 8, lambda n: chain(restart, range(1, n_q - 1), PADX + early + 8 * n, 8))
    each(n_a - 2, second_row, 2)
    wait_recv(halos_x)
    correct_border(0, frame_first)
    spread = [halo(pr, PADX, PADY, pr, d, 3) for d in (*DIRS[2:4], *DIRS[0:2], *DIRS[4:])]
    start(spread)
    third_ends(0)
    each(2, lambda t: chain(restart, range(1, n_q - 1), PADX + 4 + t * (bx - 4 - early), early - 4))
    each(2, lambda t: second_row(1 + t * (n_a - 3)))
    wait_recv(spread[:2])
    correct_middle(1, frame_again)
    wait_recv(spread[2:])
    correct_border(1, frame_again)
    third_ends(1)
    wait_send(halos_y)
    wait_send(halos_x)
    wait_send(spread)


def store(source, target, sem):
    rows = source.shape[0] // 8
    copies = [pltpu.make_async_copy(source.at[pl.ds(i * rows, rows)], target.at[pl.ds(i * rows, rows)], sem.at[i])
              for i in range(8)]
    for copy in copies:
        copy.start()
    for copy in copies:
        copy.wait()


def shards(n_sub, n_col, perm, accum, rhs, depth_x, depth_y):
    bx, by, nz = perm.shape
    ex, ey = bx + 2 * PADX, by + 2 * PADY
    field = pltpu.VMEM((ex, ey, nz), jnp.float32)
    strips_x = pltpu.VMEM((2, 8, ey, nz), jnp.float32)
    strips_y = pltpu.VMEM((2, ex, 16, nz), jnp.float32)
    hbm = pl.BlockSpec(memory_space=pl.ANY)
    vmem = pl.BlockSpec(memory_space=pltpu.VMEM)
    copies = 24 + 4 + 8
    result = pl.pallas_call(
        functools.partial(kernel, n_sub, n_col, bx, by),
        out_shape=pltpu.VMEM((bx, by, nz), jnp.float32),
        in_specs=[hbm] * 5,
        out_specs=vmem,
        scratch_shapes=[
            pltpu.VMEM((2, ey, nz), jnp.int32),
            pltpu.VMEM((2, ex, 8, nz), jnp.int32),
            pltpu.VMEM((2, by), jnp.int32),
            pltpu.VMEM((2, bx), jnp.int32),
            pltpu.VMEM((2, 2, by), jnp.int32),
            pltpu.VMEM((2, 2, bx), jnp.int32),
        ] + [field] * 8 + [strips_x] * 3 + [strips_y] * 3 + [
            pltpu.SemaphoreType.DMA((copies,)),
            pltpu.SemaphoreType.DMA((copies,)),
            pltpu.SemaphoreType.DMA((3, bx // CHUNK)),
            pltpu.SemaphoreType.DMA((2,)),
        ],
        compiler_params=pltpu.CompilerParams(
            collective_id=0, has_side_effects=True, vmem_limit_bytes=56 * 1024 * 1024),
        cost_estimate=pl.CostEstimate(
            flops=120 * bx * by * nz, bytes_accessed=16 * bx * by * nz, transcendentals=0),
    )(perm, accum, rhs, depth_x, depth_y.T)
    return pl.pallas_call(
        store,
        out_shape=jax.ShapeDtypeStruct((bx, by, nz), jnp.float32),
        in_specs=[vmem], out_specs=hbm,
        scratch_shapes=[pltpu.SemaphoreType.DMA((8,))],
        compiler_params=pltpu.CompilerParams(vmem_limit_bytes=4 * 1024 * 1024),
    )(result)


def solution(mesh):
    placed = (
        P("sub", "col", None),
        P("sub", "col", None),
        P("sub", "col", None),
        P("sub", "col"),
        P("sub", "col"),
    )
    return jax.shard_map(
        functools.partial(shards, mesh.shape["sub"], mesh.shape["col"]),
        mesh=mesh, in_specs=placed, out_specs=P("sub", "col", None), check_vma=False
    )
```

```python
import functools

import jax
import jax.numpy as jnp
from jax import lax
from jax.experimental import pallas as pl
from jax.experimental.pallas import tpu as pltpu
from jax.sharding import PartitionSpec as P

OVL = 4
VERTICAL = 0.1
MESH = pl.DeviceIdType.MESH

PADX = 3
PADY = 8
DIRS = ((-1, 0), (1, 0), (0, -1), (0, 1), (-1, -1), (-1, 1), (1, -1), (1, 1))
CHUNK = 8


def recip(value):
    return pl.reciprocal(value, approx=True)


def harmonic(first, second):
    return first * second * recip(first + second)


def kernel(n_sub, n_col, bx, by, perm, accum, rhs, depth_x, depth_y, out,
           dx_ref, dy_ref, kx, ky, hx, hy, pm, w, r, b, fx, fy, fz, pr,
           xw, xb, xc, yw, yb, yc, ssem, rsem, lsem, dsem):
    nz = 128
    s = lax.axis_index("sub")
    k = lax.axis_index("col")
    ex, ey = bx + 2 * PADX, by + 2 * PADY
    c = pm
    n_a, n_q = bx // 8 - 1, by // 8 + 1
    x_end, y_end = PADX + bx, PADY + by

    def exists(d):
        ok = None
        for coord, step, count in ((s, d[0], n_sub), (k, d[1], n_col)):
            if step == -1:
                test = coord > 0
            elif step == 1:
                test = coord < count - 1
            else:
                continue
            ok = test if ok is None else ok & test
        return ok

    def device(d):
        return (s + d[0], k + d[1])

    own_x, own_y = pl.ds(PADX, bx), pl.ds(PADY, by)

    def local(n):
        here = pl.ds(n * CHUNK, CHUNK)
        there = pl.ds(PADX + n * CHUNK, CHUNK)
        return [pltpu.make_async_copy(src.at[here], dst.at[there, own_y, :], lsem.at[i, n])
                for i, (src, dst) in enumerate(((perm, pm), (accum, w), (rhs, r)))]

    depths = [pltpu.make_async_copy(depth_x, kx, dsem.at[0]), pltpu.make_async_copy(depth_y, ky, dsem.at[1])]
    for n in range(bx // CHUNK):
        for copy in local(n):
            copy.start()
        if n == 0:
            for copy in depths:
                copy.start()

    def each(count, body, first=0):
        def step(i, carry):
            body(i)
            return carry
        lax.fori_loop(first, count, step, 0)

    def fill(value, *refs):
        for ref in refs:
            for x0 in (0, x_end):
                ref[x0:x0 + PADX, :, :] = jnp.full((PADX, ey, nz), value, jnp.float32)

        def rows(i):
            for ref in refs:
                for y0 in (0, y_end):
                    ref[pl.ds(PADX + 8 * i, 8), y0:y0 + PADY, :] = jnp.full((8, PADY, nz), value, jnp.float32)
        each(bx // 8, rows)

    fill(1e-30, pm)
    fill(1.0, w)
    fill(0.0, r, pr)
    hx[...] = jnp.zeros(hx.shape, jnp.int32)
    hy[...] = jnp.zeros(hy.shape, jnp.int32)

    barrier = pltpu.get_barrier_semaphore()
    arrivals = jnp.int32(0)
    for d in DIRS:
        @pl.when(exists(d))
        def _(d=d):
            pl.semaphore_signal(barrier, inc=1, device_id=device(d), device_id_type=MESH)
        arrivals = arrivals + jnp.where(exists(d), 1, 0).astype(jnp.int32)
    pl.semaphore_wait(barrier, arrivals)

    counter = [0]

    def remote(src, dst, d):
        i = counter[0]
        counter[0] += 1
        return d, pltpu.make_async_remote_copy(
            src_ref=src, dst_ref=dst, send_sem=ssem.at[i], recv_sem=rsem.at[i],
            device_id=device(d), device_id_type=MESH)

    def start(copies):
        for d, copy in copies:
            pl.when(exists(d))(copy.start)

    def wait_recv(copies):
        for d, copy in copies:
            pl.when(exists((-d[0], -d[1])))(copy.wait_recv)

    def wait_send(copies):
        for d, copy in copies:
            pl.when(exists(d))(copy.wait_send)

    def halo(src, ox, oy, dst, d, width):
        def span(step, offset, extent, pad, thick):
            if step == 0:
                return pl.ds(offset, extent), pl.ds(pad, extent)
            if step == 1:
                return pl.ds(offset + extent - thick, thick), pl.ds(pad - thick, thick)
            return pl.ds(offset, thick), pl.ds(pad + extent, thick)

        sxs, dxs = span(d[0], ox, bx, PADX, width)
        sys_, dys = span(d[1], oy, by, PADY, width)
        return remote(src.at[sxs, sys_, :], dst.at[dxs, dys, :], d)

    def given(d):
        return [halo(perm, 0, 0, pm, d, 3), halo(accum, 0, 0, w, d, 2), halo(rhs, 0, 0, r, d, 2)]

    halos_x = [copy for pair in zip(given(DIRS[0]), given(DIRS[1])) for copy in pair]
    halos_y = [copy for pair in zip(given(DIRS[2]), given(DIRS[3])) for copy in pair]
    halos_x += [remote(depth_y, hy.at[0], (1, 0)), remote(depth_y, hy.at[1], (-1, 0)),
                remote(depth_x, hx.at[0], (0, 1)), remote(depth_x, hx.at[1], (0, -1))]
    halos_x += [copy for d in DIRS[4:] for copy in given(d)]
    start(halos_y)
    start(halos_x)

    for ref in (xb, xc):
        ref[0, 6:8] = jnp.zeros((2, ey, nz), jnp.float32)
        ref[1, 0:2] = jnp.zeros((2, ey, nz), jnp.float32)

    def clear(i):
        for ref in (yw, yb, yc):
            for u in range(2):
                ref[u, pl.ds(i * 10, 10), 8 - 8 * u:16 - 8 * u] = jnp.zeros((10, 8, nz), jnp.float32)
    each(ex // 10, clear)
    for u in range(2):
        for x in (PADX - 1, x_end):
            yc[u, x] = jnp.zeros((16, nz), jnp.float32)

    for copy in depths:
        copy.wait()
    dx_ref[...] = jnp.zeros(dx_ref.shape, jnp.int32)
    dy_ref[...] = jnp.zeros(dy_ref.shape, jnp.int32)
    for side in range(2):
        dx_ref[side, own_y, :] = jnp.broadcast_to(kx[side:side + 1, :], (nz, by)).T
        lanes = jnp.broadcast_to(ky[side:side + 1, :], (nz, bx)).T
        dy_ref[side, own_x] = jnp.broadcast_to(lanes[:, None, :], (bx, 8, nz))

    def at(ref, x, y0):
        return ref[x, pl.ds(y0, 8), :]

    def put(ref, x, y0, value):
        ref[x, pl.ds(y0, 8), :] = value

    def strip_x(t):
        return PADX - 2 + t * (bx - 4)

    def strip_y(u):
        return PADY - 4 + u * (by - 8)

    sublane = lax.broadcasted_iota(jnp.int32, (8, nz), 0)
    lane = lax.broadcasted_iota(jnp.int32, (8, nz), 1)

    def stencil(ref, x0, y0, rows, emit, following=None, lx=0, ly=0):
        before, centre = at(ref, x0 - lx - 1, y0 - ly), at(ref, x0 - lx, y0 - ly)
        face = at(fx, x0 - 1, y0)
        backs = []
        for i in range(rows):
            x = x0 + i
            after = at(ref, x - lx + 1, y0 - ly)
            total = face * before
            face = at(fx, x, y0)
            total = total + face * after
            low = at(fy, x, y0)
            total = total + low * at(ref, x - lx, y0 - ly - 1)
            back = pltpu.roll(low * centre, 7, 0)
            if following is None:
                total = total + at(fy, x, y0 + 1) * at(ref, x - lx, y0 - ly + 1)
            else:
                total = total + jnp.where(sublane == 7, following[i], back)
            up = at(fz, x, y0)
            total = total + up * pltpu.roll(centre, nz - 1, 1)
            total = total + pltpu.roll(up * centre, 1, 1)
            emit(i, total, centre)
            backs.append(back)
            before, centre = centre, after
        return backs

    def coefficients(x0, y0, rows, emit, following=None):
        before, centre = 2.0 * at(pm, x0 - 1, y0), 2.0 * at(pm, x0, y0)
        face = harmonic(before, centre)
        put(fx, x0 - 1, y0, face)
        lows = []
        for i in range(rows):
            x = x0 + i
            after = 2.0 * at(pm, x + 1, y0)
            faces = face
            face = harmonic(centre, after)
            put(fx, x, y0, face)
            faces = faces + face
            low = harmonic(2.0 * at(pm, x, y0 - 1), centre)
            put(fy, x, y0, low)
            if following is None:
                high = harmonic(centre, 2.0 * at(pm, x, y0 + 1))
            else:
                high = pltpu.roll(jnp.where(sublane == 0, following[i], low), 7, 0)
            faces = faces + low + high
            scale = jnp.where(lane < nz - 1, jnp.float32(VERTICAL), 0.0)
            up = scale * harmonic(centre, pltpu.roll(centre, nz - 1, 1))
            put(fz, x, y0, up)
            faces = faces + up + pltpu.roll(up, 1, 1)
            emit(i, recip(at(w, x, y0) + faces))
            lows.append(low)
            centre = after
        return lows

    def end_y(t, u):
        return jnp.where(t == 0, hy[0, pl.ds(u, 1), bx - 1:bx], hy[1, pl.ds(u, 1), 0:1])

    def end_x(u, t):
        return jnp.where(u == 0, hx[0, pl.ds(t, 1), by - 1:by], hx[1, pl.ds(t, 1), 0:1])

    def strips(x0, y0, t, u):
        found = []
        if t is not None:
            found.append((xw.at[t], xb.at[t], x0 - strip_x(t), y0))
        if u is not None:
            found.append((yw.at[u], yb.at[u], x0, y0 - strip_y(u)))
        return found

    def frame_first(x0, y0, rows, t, u, ring=False):
        j = y0 - PADY + sublane
        in_y = (j >= 0) & (j < by)
        if t is not None:
            deep_x = dx_ref[t, pl.ds(y0, 8), :]
        if u is not None:
            m_y = jnp.where(u == 0, j, by - 1 - j)
        if ring and t is not None and u is not None:
            corner_x = (m_y == -1) & (end_y(t, u) >= 1)
            corner_y = (m_y == -1) & (end_x(u, t) >= 1)

        def emit(n, inverse):
            x = x0 + n
            i = x - PADX
            source = at(r, x, y0)
            if t is None:
                member = in_y
            else:
                m = jnp.where(t == 0, i, bx - 1 - i)
                beyond = m < 0
                member = jnp.where(beyond, -1 - m, jnp.where(in_y, -1, 8)) < deep_x
                other = jnp.where(beyond, jnp.where(in_y, -1, 8), m) < deep_x
                if ring and u is not None:
                    other = other | (corner_x & (m == -1))
                weight = jnp.where(other, inverse, 0.0)
                put(xw.at[t], x - strip_x(t), y0, weight)
                put(xb.at[t], x - strip_x(t), y0, weight * source)
            if u is not None:
                deep_y = dy_ref[u, x]
                inside = jnp.where((i >= 0) & (i < bx), 0, 8)
                member = member | (jnp.where(m_y < 0, -1 - m_y, 8) < deep_y)
                other = jnp.where(m_y < 0, inside - 1, m_y) < deep_y
                if ring and t is not None:
                    other = other | (corner_y & (m == -1))
                weight = jnp.where(other, inverse, 0.0)
                put(yw.at[u], x, y0 - strip_y(u), weight)
                put(yb.at[u], x, y0 - strip_y(u), weight * source)
            weight = jnp.where(member, inverse, 0.0)
            put(w, x, y0, weight)
            put(b, x, y0, weight * source)
        coefficients(x0, y0, rows, emit)

    def frame_again(x0, y0, rows, t, u, ring=False):
        def emit(n, total, centre):
            x = x0 + n
            total = at(r, x, y0) + total
            for weights, target, x1, y1 in [(w, b, x0, y0)] + strips(x0, y0, t, u):
                weight = at(weights, x1 + n, y1)
                put(target, x1 + n, y1, jnp.where(weight > 0.0, weight * total - centre, 0.0))
        stencil(pr, x0, y0, rows, emit)

    def row(a):
        return PADX + 4 + 8 * a

    def column(q):
        return PADY - 4 + 8 * q

    def frame_x(block, ring):
        def first(t):
            return PADX - 2 + t * (bx + 1) if ring else PADX + 1 + t * (bx - 5)

        def along_x(t):
            for q in range(1, n_q - 1):
                block(first(t), column(q), 3, t, None, ring)
        each(2, along_x)

        def corner(n):
            t, u = n // 2, n % 2
            block(first(t), column(u * (n_q - 1)), 3, t, u, ring)
        each(4, corner)

    def frame_y(block):
        def along_y(u):
            for a in range(n_a):
                block(row(a), column(u * (n_q - 1)), 8, None, u)
        each(2, along_y)

    def chain(body, columns, *args):
        following = None
        for q in reversed(columns):
            following = body(*args, q, following)

    def second(x0, rows, q, following):
        y0 = column(q)

        def emit(i, total, centre):
            put(c, x0 + i, y0, centre + at(w, x0 + i, y0) * total)
        return stencil(b, x0, y0, rows, emit, following)

    def second_inner():
        each(n_a - 2, lambda a: chain(second, range(2, n_q - 2), row(a + 1), 8))

    def second_ends():
        def ends(a):
            chain(second, range(n_q - 2, n_q), row(a + 1), 8)
            chain(second, range(0, 2), row(a + 1), 8)
        each(n_a - 2, ends)

    def second_next():
        each(2, lambda t: chain(second, range(n_q), PADX + 4 + t * (bx - 16), 8))

    def second_rows():
        each(2, lambda t: chain(second, range(n_q), PADX - 1 + t * (bx - 3), 5))

    def strip(src, dst, weight, x0, y0, rows, following, lx, ly):
        def emit(i, total, centre):
            x, y = x0 - lx + i, y0 - ly
            put(dst, x, y, centre + at(weight, x, y) * total)
        return stencil(src, x0, y0, rows, emit, following, lx, ly)

    def strips_along_x():
        def along_x(t):
            def block(q, following):
                return strip(xb.at[t], xc.at[t], xw.at[t], PADX - 1 + t * (bx - 3), column(q), 5, following, strip_x(t), 0)
            chain(block, range(n_q))
        each(2, along_x)

    def strips_along_y(*rows):
        def along_y(u):
            for a in rows:
                strip(yb.at[u], yc.at[u], yw.at[u], PADX + 8 * a, PADY - 3 + u * (by - 2), 8, None, 0, strip_y(u))
        each(2, along_y)

    def finish(turn, x, y0, value):
        if turn == 0:
            put(pr, x, y0, value)
        else:
            put(out, x - PADX, y0 - PADY, at(pr, x, y0) + value)

    def third_inner(turn):
        def block(x0, q, following):
            y0 = PADY + 8 * q

            def emit(i, total, centre):
                x = x0 + i
                finish(turn, x, y0, at(b, x, y0) + at(w, x, y0) * total)
            return stencil(c, x0, y0, 8, emit, following)
        return lambda a: chain(block, range(1, by // 8 - 1), row(a))

    def border(turn, x0, y0, rows, t, u, following=(None, None)):
        sums, covers, backs = [None] * rows, [None] * rows, []

        def add(i, value, weight):
            sums[i] = value if sums[i] is None else sums[i] + value
            if weight is not None:
                covers[i] = jnp.where(weight > 0.0, 2.0 if covers[i] is None else covers[i] + 1.0,
                                      1.0 if covers[i] is None else covers[i])

        def own(i, total, centre):
            add(i, at(b, x0 + i, y0) + at(w, x0 + i, y0) * total, None)
        backs.append(stencil(c, x0, y0, rows, own, following[0]))
        for n, (weights, source, x1, y1) in enumerate(strips(x0, y0, t, u)):
            def other(i, total, centre, weights=weights, source=source, x1=x1, y1=y1):
                weight = at(weights, x1 + i, y1)
                add(i, at(source, x1 + i, y1) + weight * total, weight)
            along_x = t is not None and n == 0
            backs.append(stencil(xc.at[t] if along_x else yc.at[u], x0, y0, rows, other,
                                 following[1] if along_x else None, x0 - x1, y0 - y1))
        for i in range(rows):
            finish(turn, x0 + i, y0, sums[i] * recip(covers[i]))
        return backs

    def border_x(turn):
        def corner(n):
            t, u = n // 2, n % 2
            border(turn, PADX + t * (bx - 4), PADY + u * (by - 8), 4, t, u)
        each(4, corner)

        def along_x(t):
            following = (None, None)
            for q in reversed(range(1, by // 8 - 1)):
                following = border(turn, PADX + t * (bx - 4), PADY + 8 * q, 4, t, None, following)
        each(2, along_x)

    def border_y(turn, *rows):
        def along_y(u):
            for a in rows:
                border(turn, row(a), PADY + u * (by - 8), 8, None, u)
        each(2, along_y)

    for copy in local(0):
        copy.wait()

    def first_row(a):
        for copy in local(a + 1):
            copy.wait()

        def block(x0, q, following):
            y0 = column(q)

            def emit(i, inverse):
                put(w, x0 + i, y0, inverse)
                put(b, x0 + i, y0, inverse * at(r, x0 + i, y0))
            return coefficients(x0, y0, 8, emit, following)
        chain(block, range(1, n_q - 1), row(a))
    each(n_a, first_row)
    middle = range(2, n_a - 2)
    ends = [a for a in range(n_a) if a not in middle]

    def correct(turn, frame, along_y, along_x):
        second_inner()
        wait_recv(along_y)
        frame_y(frame)
        frame_x(frame, False)
        second_ends()
        second_next()
        strips_along_y(*range(1, bx // 8 - 1))
        border_y(turn, *middle)
        each(n_a - 2, third_inner(turn), 2)
        wait_recv(along_x)
        frame_x(frame, True)
        second_rows()
        strips_along_x()
        strips_along_y(0, bx // 8 - 1)
        border_x(turn)
        border_y(turn, *ends)

    def third_ends(turn):
        each(4, lambda n: third_inner(turn)(n + (n // 2) * (n_a - 4)))

    correct(0, frame_first, halos_y, halos_x)
    spread = [halo(pr, PADX, PADY, pr, d, 3) for d in (*DIRS[2:4], *DIRS[0:2], *DIRS[4:])]
    start(spread)
    third_ends(0)

    def restart(x0, q, following):
        y0 = column(q)

        def emit(i, total, centre):
            x = x0 + i
            put(b, x, y0, at(w, x, y0) * (at(r, x, y0) + total) - centre)
        return stencil(pr, x0, y0, 8, emit, following)
    each(n_a, lambda a: chain(restart, range(1, n_q - 1), row(a)))
    correct(1, frame_again, spread[:2], spread[2:])
    third_ends(1)
    wait_send(halos_y)
    wait_send(halos_x)
    wait_send(spread)


def store(source, target, sem):
    rows = source.shape[0] // 8
    copies = [pltpu.make_async_copy(source.at[pl.ds(i * rows, rows)], target.at[pl.ds(i * rows, rows)], sem.at[i])
              for i in range(8)]
    for copy in copies:
        copy.start()
    for copy in copies:
        copy.wait()


def shards(n_sub, n_col, perm, accum, rhs, depth_x, depth_y):
    bx, by, nz = perm.shape
    ex, ey = bx + 2 * PADX, by + 2 * PADY
    field = pltpu.VMEM((ex, ey, nz), jnp.float32)
    strips_x = pltpu.VMEM((2, 8, ey, nz), jnp.float32)
    strips_y = pltpu.VMEM((2, ex, 16, nz), jnp.float32)
    hbm = pl.BlockSpec(memory_space=pl.ANY)
    vmem = pl.BlockSpec(memory_space=pltpu.VMEM)
    copies = 24 + 4 + 8
    result = pl.pallas_call(
        functools.partial(kernel, n_sub, n_col, bx, by),
        out_shape=pltpu.VMEM((bx, by, nz), jnp.float32),
        in_specs=[hbm] * 5,
        out_specs=vmem,
        scratch_shapes=[
            pltpu.VMEM((2, ey, nz), jnp.int32),
            pltpu.VMEM((2, ex, 8, nz), jnp.int32),
            pltpu.VMEM((2, by), jnp.int32),
            pltpu.VMEM((2, bx), jnp.int32),
            pltpu.VMEM((2, 2, by), jnp.int32),
            pltpu.VMEM((2, 2, bx), jnp.int32),
        ] + [field] * 8 + [strips_x] * 3 + [strips_y] * 3 + [
            pltpu.SemaphoreType.DMA((copies,)),
            pltpu.SemaphoreType.DMA((copies,)),
            pltpu.SemaphoreType.DMA((3, bx // CHUNK)),
            pltpu.SemaphoreType.DMA((2,)),
        ],
        compiler_params=pltpu.CompilerParams(
            collective_id=0, has_side_effects=True, vmem_limit_bytes=56 * 1024 * 1024),
        cost_estimate=pl.CostEstimate(
            flops=120 * bx * by * nz, bytes_accessed=16 * bx * by * nz, transcendentals=0),
    )(perm, accum, rhs, depth_x, depth_y.T)
    return pl.pallas_call(
        store,
        out_shape=jax.ShapeDtypeStruct((bx, by, nz), jnp.float32),
        in_specs=[vmem], out_specs=hbm,
        scratch_shapes=[pltpu.SemaphoreType.DMA((8,))],
        compiler_params=pltpu.CompilerParams(vmem_limit_bytes=4 * 1024 * 1024),
    )(result)


def solution(mesh):
    placed = (
        P("sub", "col", None),
        P("sub", "col", None),
        P("sub", "col", None),
        P("sub", "col"),
        P("sub", "col"),
    )
    return jax.shard_map(
        functools.partial(shards, mesh.shape["sub"], mesh.shape["col"]),
        mesh=mesh, in_specs=placed, out_specs=P("sub", "col", None), check_vma=False
    )
```

```python
import functools

import jax
import jax.numpy as jnp
from jax import lax
from jax.experimental import pallas as pl
from jax.experimental.pallas import tpu as pltpu
from jax.sharding import PartitionSpec as P

OVL = 4
VERTICAL = 0.1
MESH = pl.DeviceIdType.MESH

PADX = 3
PADY = 8
DIRS = ((-1, 0), (1, 0), (0, -1), (0, 1), (-1, -1), (-1, 1), (1, -1), (1, 1))
CHUNK = 8


def recip(value):
    return pl.reciprocal(value, approx=True)


def harmonic(first, second):
    return first * second * recip(first + second)


def kernel(n_sub, n_col, bx, by, perm, accum, rhs, depth_x, depth_y, out,
           dx_ref, dy_ref, kx, ky, hx, hy, pm, w, r, b, fx, fy, fz, pr,
           xw, xb, xc, yw, yb, yc, ssem, rsem, lsem, dsem):
    nz = 128
    s = lax.axis_index("sub")
    k = lax.axis_index("col")
    ex, ey = bx + 2 * PADX, by + 2 * PADY
    c = pm
    n_a, n_q = bx // 8 - 1, by // 8 + 1
    x_end, y_end = PADX + bx, PADY + by

    def exists(d):
        ok = None
        for coord, step, count in ((s, d[0], n_sub), (k, d[1], n_col)):
            if step == -1:
                test = coord > 0
            elif step == 1:
                test = coord < count - 1
            else:
                continue
            ok = test if ok is None else ok & test
        return ok

    def device(d):
        return (s + d[0], k + d[1])

    own_x, own_y = pl.ds(PADX, bx), pl.ds(PADY, by)

    def local(n):
        here = pl.ds(n * CHUNK, CHUNK)
        there = pl.ds(PADX + n * CHUNK, CHUNK)
        return [pltpu.make_async_copy(src.at[here], dst.at[there, own_y, :], lsem.at[i, n])
                for i, (src, dst) in enumerate(((perm, pm), (accum, w), (rhs, r)))]

    depths = [pltpu.make_async_copy(depth_x, kx, dsem.at[0]), pltpu.make_async_copy(depth_y, ky, dsem.at[1])]
    for n in range(bx // CHUNK):
        for copy in local(n):
            copy.start()
        if n == 0:
            for copy in depths:
                copy.start()

    def each(count, body, first=0):
        def step(i, carry):
            body(i)
            return carry
        lax.fori_loop(first, count, step, 0)

    def fill(value, *refs):
        for ref in refs:
            for x0 in (0, x_end):
                ref[x0:x0 + PADX, :, :] = jnp.full((PADX, ey, nz), value, jnp.float32)

        def rows(i):
            for ref in refs:
                for y0 in (0, y_end):
                    ref[pl.ds(PADX + 8 * i, 8), y0:y0 + PADY, :] = jnp.full((8, PADY, nz), value, jnp.float32)
        each(bx // 8, rows)

    fill(1e-30, pm)
    fill(1.0, w)
    fill(0.0, r, pr)
    hx[...] = jnp.zeros(hx.shape, jnp.int32)
    hy[...] = jnp.zeros(hy.shape, jnp.int32)

    barrier = pltpu.get_barrier_semaphore()
    arrivals = jnp.int32(0)
    for d in DIRS:
        @pl.when(exists(d))
        def _(d=d):
            pl.semaphore_signal(barrier, inc=1, device_id=device(d), device_id_type=MESH)
        arrivals = arrivals + jnp.where(exists(d), 1, 0).astype(jnp.int32)
    pl.semaphore_wait(barrier, arrivals)

    counter = [0]

    def remote(src, dst, d):
        i = counter[0]
        counter[0] += 1
        return d, pltpu.make_async_remote_copy(
            src_ref=src, dst_ref=dst, send_sem=ssem.at[i], recv_sem=rsem.at[i],
            device_id=device(d), device_id_type=MESH)

    def start(copies):
        for d, copy in copies:
            pl.when(exists(d))(copy.start)

    def wait_recv(copies):
        for d, copy in copies:
            pl.when(exists((-d[0], -d[1])))(copy.wait_recv)

    def wait_send(copies):
        for d, copy in copies:
            pl.when(exists(d))(copy.wait_send)

    def halo(src, ox, oy, dst, d, width):
        def span(step, offset, extent, pad, thick):
            if step == 0:
                return pl.ds(offset, extent), pl.ds(pad, extent)
            if step == 1:
                return pl.ds(offset + extent - thick, thick), pl.ds(pad - thick, thick)
            return pl.ds(offset, thick), pl.ds(pad + extent, thick)

        sxs, dxs = span(d[0], ox, bx, PADX, width)
        sys_, dys = span(d[1], oy, by, PADY, width)
        return remote(src.at[sxs, sys_, :], dst.at[dxs, dys, :], d)

    def given(d):
        return [halo(perm, 0, 0, pm, d, 3), halo(accum, 0, 0, w, d, 2), halo(rhs, 0, 0, r, d, 2)]

    halos_x = [copy for pair in zip(given(DIRS[0]), given(DIRS[1])) for copy in pair]
    halos_y = [copy for pair in zip(given(DIRS[2]), given(DIRS[3])) for copy in pair]
    halos_x += [remote(depth_y, hy.at[0], (1, 0)), remote(depth_y, hy.at[1], (-1, 0)),
                remote(depth_x, hx.at[0], (0, 1)), remote(depth_x, hx.at[1], (0, -1))]
    halos_x += [copy for d in DIRS[4:] for copy in given(d)]
    start(halos_y)
    start(halos_x)

    for ref in (xb, xc):
        ref[0, 6:8] = jnp.zeros((2, ey, nz), jnp.float32)
        ref[1, 0:2] = jnp.zeros((2, ey, nz), jnp.float32)

    def clear(i):
        for ref in (yw, yb, yc):
            for u in range(2):
                ref[u, pl.ds(i * 10, 10), 8 - 8 * u:16 - 8 * u] = jnp.zeros((10, 8, nz), jnp.float32)
    each(ex // 10, clear)
    for u in range(2):
        for x in (PADX - 1, x_end):
            yc[u, x] = jnp.zeros((16, nz), jnp.float32)

    for copy in depths:
        copy.wait()
    dx_ref[...] = jnp.zeros(dx_ref.shape, jnp.int32)
    dy_ref[...] = jnp.zeros(dy_ref.shape, jnp.int32)
    for side in range(2):
        dx_ref[side, own_y, :] = jnp.broadcast_to(kx[side:side + 1, :], (nz, by)).T
        lanes = jnp.broadcast_to(ky[side:side + 1, :], (nz, bx)).T
        dy_ref[side, own_x] = jnp.broadcast_to(lanes[:, None, :], (bx, 8, nz))

    def at(ref, x, y0):
        return ref[x, pl.ds(y0, 8), :]

    def put(ref, x, y0, value):
        ref[x, pl.ds(y0, 8), :] = value

    def strip_x(t):
        return PADX - 2 + t * (bx - 4)

    def strip_y(u):
        return PADY - 4 + u * (by - 8)

    sublane = lax.broadcasted_iota(jnp.int32, (8, nz), 0)
    lane = lax.broadcasted_iota(jnp.int32, (8, nz), 1)

    def stencil(ref, x0, y0, rows, emit, following=None, lx=0, ly=0):
        before, centre = at(ref, x0 - lx - 1, y0 - ly), at(ref, x0 - lx, y0 - ly)
        face = at(fx, x0 - 1, y0)
        backs = []
        for i in range(rows):
            x = x0 + i
            after = at(ref, x - lx + 1, y0 - ly)
            total = face * before
            face = at(fx, x, y0)
            total = total + face * after
            low = at(fy, x, y0)
            total = total + low * at(ref, x - lx, y0 - ly - 1)
            back = pltpu.roll(low * centre, 7, 0)
            if following is None:
                total = total + at(fy, x, y0 + 1) * at(ref, x - lx, y0 - ly + 1)
            else:
                total = total + jnp.where(sublane == 7, following[i], back)
            up = at(fz, x, y0)
            total = total + up * pltpu.roll(centre, nz - 1, 1)
            total = total + pltpu.roll(up * centre, 1, 1)
            emit(i, total, centre)
            backs.append(back)
            before, centre = centre, after
        return backs

    def coefficients(x0, y0, rows, emit, following=None):
        before, centre = 2.0 * at(pm, x0 - 1, y0), 2.0 * at(pm, x0, y0)
        face = harmonic(before, centre)
        put(fx, x0 - 1, y0, face)
        lows = []
        for i in range(rows):
            x = x0 + i
            after = 2.0 * at(pm, x + 1, y0)
            faces = face
            face = harmonic(centre, after)
            put(fx, x, y0, face)
            faces = faces + face
            low = harmonic(2.0 * at(pm, x, y0 - 1), centre)
            put(fy, x, y0, low)
            if following is None:
                high = harmonic(centre, 2.0 * at(pm, x, y0 + 1))
            else:
                high = pltpu.roll(jnp.where(sublane == 0, following[i], low), 7, 0)
            faces = faces + low + high
            scale = jnp.where(lane < nz - 1, jnp.float32(VERTICAL), 0.0)
            up = scale * harmonic(centre, pltpu.roll(centre, nz - 1, 1))
            put(fz, x, y0, up)
            faces = faces + up + pltpu.roll(up, 1, 1)
            emit(i, recip(at(w, x, y0) + faces))
            lows.append(low)
            centre = after
        return lows

    def end_y(t, u):
        return jnp.where(t == 0, hy[0, pl.ds(u, 1), bx - 1:bx], hy[1, pl.ds(u, 1), 0:1])

    def end_x(u, t):
        return jnp.where(u == 0, hx[0, pl.ds(t, 1), by - 1:by], hx[1, pl.ds(t, 1), 0:1])

    def strips(x0, y0, t, u):
        found = []
        if t is not None:
            found.append((xw.at[t], xb.at[t], x0 - strip_x(t), y0))
        if u is not None:
            found.append((yw.at[u], yb.at[u], x0, y0 - strip_y(u)))
        return found

    def frame_first(x0, y0, rows, t, u, ring=False):
        j = y0 - PADY + sublane
        in_y = (j >= 0) & (j < by)
        if t is not None:
            deep_x = dx_ref[t, pl.ds(y0, 8), :]
        if u is not None:
            m_y = jnp.where(u == 0, j, by - 1 - j)
        if ring and t is not None and u is not None:
            corner_x = (m_y == -1) & (end_y(t, u) >= 1)
            corner_y = (m_y == -1) & (end_x(u, t) >= 1)

        def emit(n, inverse):
            x = x0 + n
            i = x - PADX
            source = at(r, x, y0)
            if t is None:
                member = in_y
            else:
                m = jnp.where(t == 0, i, bx - 1 - i)
                beyond = m < 0
                member = jnp.where(beyond, -1 - m, jnp.where(in_y, -1, 8)) < deep_x
                other = jnp.where(beyond, jnp.where(in_y, -1, 8), m) < deep_x
                if ring and u is not None:
                    other = other | (corner_x & (m == -1))
                weight = jnp.where(other, inverse, 0.0)
                put(xw.at[t], x - strip_x(t), y0, weight)
                put(xb.at[t], x - strip_x(t), y0, weight * source)
            if u is not None:
                deep_y = dy_ref[u, x]
                inside = jnp.where((i >= 0) & (i < bx), 0, 8)
                member = member | (jnp.where(m_y < 0, -1 - m_y, 8) < deep_y)
                other = jnp.where(m_y < 0, inside - 1, m_y) < deep_y
                if ring and t is not None:
                    other = other | (corner_y & (m == -1))
                weight = jnp.where(other, inverse, 0.0)
                put(yw.at[u], x, y0 - strip_y(u), weight)
                put(yb.at[u], x, y0 - strip_y(u), weight * source)
            weight = jnp.where(member, inverse, 0.0)
            put(w, x, y0, weight)
            put(b, x, y0, weight * source)
        coefficients(x0, y0, rows, emit)

    def frame_again(x0, y0, rows, t, u, ring=False):
        def emit(n, total, centre):
            x = x0 + n
            total = at(r, x, y0) + total
            for weights, target, x1, y1 in [(w, b, x0, y0)] + strips(x0, y0, t, u):
                weight = at(weights, x1 + n, y1)
                put(target, x1 + n, y1, jnp.where(weight > 0.0, weight * total - centre, 0.0))
        stencil(pr, x0, y0, rows, emit)

    def row(a):
        return PADX + 4 + 8 * a

    def column(q):
        return PADY - 4 + 8 * q

    def frame_x(block, ring):
        def first(t):
            return PADX - 2 + t * (bx + 1) if ring else PADX + 1 + t * (bx - 5)

        def along_x(t):
            for q in range(1, n_q - 1):
                block(first(t), column(q), 3, t, None, ring)
        each(2, along_x)

        def corner(n):
            t, u = n // 2, n % 2
            block(first(t), column(u * (n_q - 1)), 3, t, u, ring)
        each(4, corner)

    def frame_y(block):
        def along_y(u):
            for a in range(n_a):
                block(row(a), column(u * (n_q - 1)), 8, None, u)
        each(2, along_y)

    def chain(body, columns, *args):
        following = None
        for q in reversed(columns):
            following = body(*args, q, following)

    def second(x0, rows, q, following):
        y0 = column(q)

        def emit(i, total, centre):
            put(c, x0 + i, y0, centre + at(w, x0 + i, y0) * total)
        return stencil(b, x0, y0, rows, emit, following)

    def second_inner():
        each(n_a - 2, lambda a: chain(second, range(2, n_q - 2), row(a + 1), 8))

    def second_ends():
        def ends(a):
            chain(second, range(n_q - 2, n_q), row(a + 1), 8)
            chain(second, range(0, 2), row(a + 1), 8)
        each(n_a - 2, ends)

    def second_next():
        each(2, lambda t: chain(second, range(n_q), PADX + 4 + t * (bx - 16), 8))

    def second_rows():
        each(2, lambda t: chain(second, range(n_q), PADX - 1 + t * (bx - 3), 5))

    def strip(src, dst, weight, x0, y0, rows, following, lx, ly):
        def emit(i, total, centre):
            x, y = x0 - lx + i, y0 - ly
            put(dst, x, y, centre + at(weight, x, y) * total)
        return stencil(src, x0, y0, rows, emit, following, lx, ly)

    def strips_along_x():
        def along_x(t):
            def block(q, following):
                return strip(xb.at[t], xc.at[t], xw.at[t], PADX - 1 + t * (bx - 3), column(q), 5, following, strip_x(t), 0)
            chain(block, range(n_q))
        each(2, along_x)

    def strips_along_y(*rows):
        def along_y(u):
            for a in rows:
                strip(yb.at[u], yc.at[u], yw.at[u], PADX + 8 * a, PADY - 3 + u * (by - 2), 8, None, 0, strip_y(u))
        each(2, along_y)

    def finish(turn, x, y0, value):
        if turn == 0:
            put(pr, x, y0, value)
        else:
            put(out, x - PADX, y0 - PADY, at(pr, x, y0) + value)

    def third_inner(turn):
        def block(x0, q, following):
            y0 = PADY + 8 * q

            def emit(i, total, centre):
                x = x0 + i
                finish(turn, x, y0, at(b, x, y0) + at(w, x, y0) * total)
            return stencil(c, x0, y0, 8, emit, following)
        return lambda a: chain(block, range(1, by // 8 - 1), row(a))

    def border(turn, x0, y0, rows, t, u, following=(None, None)):
        sums, covers, backs = [None] * rows, [None] * rows, []

        def add(i, value, weight):
            sums[i] = value if sums[i] is None else sums[i] + value
            if weight is not None:
                covers[i] = jnp.where(weight > 0.0, 2.0 if covers[i] is None else covers[i] + 1.0,
                                      1.0 if covers[i] is None else covers[i])

        def own(i, total, centre):
            add(i, at(b, x0 + i, y0) + at(w, x0 + i, y0) * total, None)
        backs.append(stencil(c, x0, y0, rows, own, following[0]))
        for n, (weights, source, x1, y1) in enumerate(strips(x0, y0, t, u)):
            def other(i, total, centre, weights=weights, source=source, x1=x1, y1=y1):
                weight = at(weights, x1 + i, y1)
                add(i, at(source, x1 + i, y1) + weight * total, weight)
            along_x = t is not None and n == 0
            backs.append(stencil(xc.at[t] if along_x else yc.at[u], x0, y0, rows, other,
                                 following[1] if along_x else None, x0 - x1, y0 - y1))
        for i in range(rows):
            finish(turn, x0 + i, y0, sums[i] * recip(covers[i]))
        return backs

    def border_x(turn):
        def corner(n):
            t, u = n // 2, n % 2
            border(turn, PADX + t * (bx - 4), PADY + u * (by - 8), 4, t, u)
        each(4, corner)

        def along_x(t):
            following = (None, None)
            for q in reversed(range(1, by // 8 - 1)):
                following = border(turn, PADX + t * (bx - 4), PADY + 8 * q, 4, t, None, following)
        each(2, along_x)

    def border_y(turn, *rows):
        def along_y(u):
            for a in rows:
                border(turn, row(a), PADY + u * (by - 8), 8, None, u)
        each(2, along_y)

    for copy in local(0):
        copy.wait()

    def first_row(a):
        for copy in local(a + 1):
            copy.wait()

        def block(x0, q, following):
            y0 = column(q)

            def emit(i, inverse):
                put(w, x0 + i, y0, inverse)
                put(b, x0 + i, y0, inverse * at(r, x0 + i, y0))
            return coefficients(x0, y0, 8, emit, following)
        chain(block, range(1, n_q - 1), row(a))
    each(n_a, first_row)
    middle = range(2, n_a - 2)
    ends = [a for a in range(n_a) if a not in middle]

    def correct(turn, frame, along_y, along_x):
        second_inner()
        wait_recv(along_y)
        frame_y(frame)
        frame_x(frame, False)
        second_ends()
        second_next()
        strips_along_y(*range(1, bx // 8 - 1))
        border_y(turn, *middle)
        each(n_a - 2, third_inner(turn), 2)
        wait_recv(along_x)
        frame_x(frame, True)
        second_rows()
        strips_along_x()
        strips_along_y(0, bx // 8 - 1)
        border_x(turn)
        border_y(turn, *ends)

    def third_ends(turn):
        each(4, lambda n: third_inner(turn)(n + (n // 2) * (n_a - 4)))

    correct(0, frame_first, halos_y, halos_x)
    spread = [halo(pr, PADX, PADY, pr, d, 3) for d in (*DIRS[2:4], *DIRS[0:2], *DIRS[4:])]
    start(spread)
    third_ends(0)

    def restart(x0, q, following):
        y0 = column(q)

        def emit(i, total, centre):
            x = x0 + i
            put(b, x, y0, at(w, x, y0) * (at(r, x, y0) + total) - centre)
        return stencil(pr, x0, y0, 8, emit, following)
    each(n_a, lambda a: chain(restart, range(1, n_q - 1), row(a)))
    correct(1, frame_again, spread[:2], spread[2:])
    third_ends(1)
    wait_send(halos_y)
    wait_send(halos_x)
    wait_send(spread)


def shards(n_sub, n_col, perm, accum, rhs, depth_x, depth_y):
    bx, by, nz = perm.shape
    ex, ey = bx + 2 * PADX, by + 2 * PADY
    field = pltpu.VMEM((ex, ey, nz), jnp.float32)
    strips_x = pltpu.VMEM((2, 8, ey, nz), jnp.float32)
    strips_y = pltpu.VMEM((2, ex, 16, nz), jnp.float32)
    hbm = pl.BlockSpec(memory_space=pl.ANY)
    vmem = pl.BlockSpec(memory_space=pltpu.VMEM)
    copies = 24 + 4 + 8
    result = pl.pallas_call(
        functools.partial(kernel, n_sub, n_col, bx, by),
        out_shape=pltpu.VMEM((bx, by, nz), jnp.float32),
        in_specs=[hbm] * 5,
        out_specs=vmem,
        scratch_shapes=[
            pltpu.VMEM((2, ey, nz), jnp.int32),
            pltpu.VMEM((2, ex, 8, nz), jnp.int32),
            pltpu.VMEM((2, by), jnp.int32),
            pltpu.VMEM((2, bx), jnp.int32),
            pltpu.VMEM((2, 2, by), jnp.int32),
            pltpu.VMEM((2, 2, bx), jnp.int32),
        ] + [field] * 8 + [strips_x] * 3 + [strips_y] * 3 + [
            pltpu.SemaphoreType.DMA((copies,)),
            pltpu.SemaphoreType.DMA((copies,)),
            pltpu.SemaphoreType.DMA((3, bx // CHUNK)),
            pltpu.SemaphoreType.DMA((2,)),
        ],
        compiler_params=pltpu.CompilerParams(
            collective_id=0, has_side_effects=True, vmem_limit_bytes=56 * 1024 * 1024),
        cost_estimate=pl.CostEstimate(
            flops=120 * bx * by * nz, bytes_accessed=16 * bx * by * nz, transcendentals=0),
    )(perm, accum, rhs, depth_x, depth_y.T)
    return result


def solution(mesh):
    placed = (
        P("sub", "col", None),
        P("sub", "col", None),
        P("sub", "col", None),
        P("sub", "col"),
        P("sub", "col"),
    )
    return jax.shard_map(
        functools.partial(shards, mesh.shape["sub"], mesh.shape["col"]),
        mesh=mesh, in_specs=placed, out_specs=P("sub", "col", None), check_vma=False
    )
```
